32 devices in a mesh: ax: 2 (over x), az: 4 (over z), rad: 4 (over y, core).
Axes of the slice: x: 2, y: 2, z: 4, core: 2. Of those that a mesh axis runs over, the one named last changes fastest.
Arguments:
- velocity: float32 [512, 64, 512], P('rad', 'az', 'ax'), may hold values from -4 to 4
- radial_courant: bfloat16 [512, 64, 512], P('rad', 'az', 'ax'), may hold values from -0.5 to 0.5
- axial_courant: bfloat16 [512, 64, 512], P('rad', 'az', 'ax'), may hold values from -0.5 to 0.5
- radial_diffusion: float32 [512], P('rad'), may hold values from 2048 to 8192
Outputs:
- advanced: float32 [512, 64, 512], P('rad', 'az', 'ax')
The draws below stay inside these ranges and needn't reach their ends.
All inputs are finite; a program needn't handle non-finite values.
Results may differ from the reference program's by a relative error of at most 0.0009.
Values sent between devices are 32-bit elements; how exact they have to be, the bound alone decides.
A program may use at most 64 MiB of HBM per device.

```python
import math
import jax
import jax.numpy as jnp
from jax import lax

NR = 512
STEPS = 6
NT = 64
NZ = 512


def levels(stream_key, extent, split, smallest, largest):
    level, own = 1.0, jax.random.fold_in(stream_key, 6)
    for axis_at, blocks in split:
        steps = jnp.exp(jax.random.uniform(jax.random.fold_in(own, axis_at), (blocks,), jnp.float32, smallest / len(split), largest / len(split)))
        level = level * jnp.repeat(steps, extent[axis_at] // blocks).reshape([-1 if axis == axis_at else 1 for axis in range(len(extent))])
    return level


def noise(stream_key, shape, scale, limit, shards=(), held_as=jnp.bfloat16):
    result = scale * jax.random.normal(stream_key, shape, jnp.float32)
    if shards:
        result = result * levels(stream_key, shape, shards, -0.22, 0.18)
    return jnp.clip(result, -limit, limit).astype(held_as)


def setup_inputs(seed: int = 0) -> dict:
    keys = jax.random.split(jax.random.key(seed), 5)
    return {
        "velocity": noise(keys[0], (NR, NT, NZ), 1.0, 4.0, ((0, 4), (1, 4), (2, 2)), jnp.float32),
        "radial_courant": jnp.clip(jax.random.uniform(keys[1], (NR, NT, NZ), jnp.float32, -0.5, 0.5) * levels(keys[1], (NR, NT, NZ), ((0, 4), (1, 4), (2, 2)), -0.4, 0.0), -0.5, 0.5).astype(jnp.bfloat16),
        "axial_courant": jnp.clip(jax.random.uniform(keys[2], (NR, NT, NZ), jnp.float32, -0.5, 0.5) * levels(keys[2], (NR, NT, NZ), ((0, 4), (1, 4), (2, 2)), -0.4, 0.0), -0.5, 0.5).astype(jnp.bfloat16),
        "radial_diffusion": jnp.clip(jnp.exp(math.log(8192.0) - 1.3862944 * jax.random.uniform(keys[3], (NR,), jnp.float32) ** levels(keys[3], (NR,), ((0, 4),), -0.2, 0.2)), 2048.0, 8192.0),
    }


theta_rate = 0.25
axial_mixing = 0.25
azimuth_mixing = 0.25

def radial_terms(radial_diffusion, position):
    spacing = 1.0 / (NR + 1)
    radius = 1.0 + (position + 1.0) * spacing
    inward = radial_diffusion * (radius - 0.5 * spacing) / radius
    outward = radial_diffusion * (radius + 0.5 * spacing) / radius
    curvature = radial_diffusion * spacing * spacing / (radius * radius)
    return (radius, inward, outward, curvature)

def right_side(state_field, radial_lower, radial_upper, axial_minus_two, axial_minus_one, axial_plus_one, axial_plus_two, azimuth_minus_two, azimuth_minus_one, azimuth_plus_one, azimuth_plus_two, radial_courant, axial_courant, radius, inward, outward, curvature):
    radius_col = radius[:, None, None]
    spread = outward[:, None, None] * (radial_upper - state_field) - inward[:, None, None] * (state_field - radial_lower) - curvature[:, None, None] * state_field
    radial_slope = 0.5 * (radial_upper - radial_lower)
    axial_slope = (8.0 * (axial_plus_one - axial_minus_one) - (axial_plus_two - axial_minus_two)) / 12.0
    axial_curve = (16.0 * (axial_plus_one + axial_minus_one) - (axial_plus_two + axial_minus_two) - 30.0 * state_field) / 12.0
    azimuth_slope = (8.0 * (azimuth_plus_one - azimuth_minus_one) - (azimuth_plus_two - azimuth_minus_two)) / 12.0
    azimuth_curve = (16.0 * (azimuth_plus_one + azimuth_minus_one) - (azimuth_plus_two + azimuth_minus_two) - 30.0 * state_field) / 12.0
    transport = radial_courant * radial_slope + axial_courant * axial_slope + theta_rate * state_field * azimuth_slope / radius_col
    mixing = axial_mixing * axial_curve + azimuth_mixing * azimuth_curve / (radius_col * radius_col)
    return state_field + spread - transport + mixing

def reference(velocity, radial_courant, axial_courant, radial_diffusion):
    position = jnp.arange(NR).astype(radial_diffusion.dtype)
    radius, inward, outward, curvature = radial_terms(radial_diffusion, position)
    zero_one = jnp.zeros((1,), radial_diffusion.dtype)
    lower_diag = jnp.concatenate([zero_one, -inward[1:]])
    upper_diag = jnp.concatenate([-outward[:-1], zero_one])
    main_diag = 1.0 + inward + outward + curvature
    state_field = velocity
    for turn_index in range(STEPS):
        padded_radial = jnp.pad(state_field, ((1, 1), (0, 0), (0, 0)))
        padded_axial = jnp.pad(state_field, ((0, 0), (0, 0), (2, 2)))
        right_hand = right_side(state_field, padded_radial[:-2], padded_radial[2:], padded_axial[:, :, :-4], padded_axial[:, :, 1:-3], padded_axial[:, :, 3:-1], padded_axial[:, :, 4:], jnp.roll(state_field, 2, axis=1), jnp.roll(state_field, 1, axis=1), jnp.roll(state_field, -1, axis=1), jnp.roll(state_field, -2, axis=1), radial_courant, axial_courant, radius, inward, outward, curvature)
        solved = lax.linalg.tridiagonal_solve(lower_diag, main_diag, upper_diag, right_hand.reshape(NR, -1))
        state_field = solved.reshape(state_field.shape)
    return state_field
```

```python
import functools

import jax
import jax.numpy as jnp
from jax import lax
from jax.experimental import pallas as pl
from jax.experimental.pallas import tpu as pltpu
from jax.sharding import PartitionSpec as P

NR = 512
STEPS = 6
F32 = jnp.float32
MESH = pl.DeviceIdType.MESH
PAD = 8
CH = 16


def join_slabs(left, right):
    head_l, tail_l, tl = left
    head_r, tail_r, tr = right
    divisor = 1.0 - tl[3] * tr[0]
    mid_value = (tail_l - tl[3] * head_r) / divisor
    mid_left = tl[2] / divisor
    mid_right = -tl[3] * tr[1] / divisor
    next_value = head_r - tr[0] * mid_value
    next_left = -tr[0] * mid_left
    next_right = tr[1] - tr[0] * mid_right
    return (
        head_l - tl[1] * next_value,
        tail_r - tr[2] * mid_value,
        (
            tl[0] - tl[1] * next_left,
            -tl[1] * next_right,
            -tr[2] * mid_left,
            tr[3] - tr[2] * mid_right,
        ),
    )


def interface_rows(members, me, n):
    zero = jnp.zeros_like(members[0][0])
    identity = (zero, zero, (zero, zero - 1.0, zero - 1.0, zero))

    def choose(cond, a, b):
        return jax.tree.map(lambda x, y: jnp.where(cond, x, y), a, b)

    prefix = identity
    own = members[0]
    for k in range(n):
        own = choose(k == me, members[k], own)
        prefix = choose(k < me, join_slabs(prefix, members[k]), prefix)
    suffix = identity
    for k in range(n - 1, -1, -1):
        suffix = choose(k > me, join_slabs(members[k], suffix), suffix)
    combined = join_slabs(own, suffix)
    lower = (prefix[1] - prefix[2][3] * combined[0]) / (1.0 - prefix[2][3] * combined[2][0])
    upper = (suffix[0] - suffix[2][0] * (own[1] - own[2][2] * lower)) / (
        1.0 - suffix[2][0] * own[2][3]
    )
    return lower, upper


SCALE = 48.0


def kernel(
    n, naz, R, NTL, NZL,
    v, rc, ac, rd, out,
    F, FB, HA, Y, YE, Q, QE, SC, SCE, RCF, ACF, BW, PS, PR, RB0, RBE, RBI, TB, MA, MB, KC,
    PHI, PSI, DP, DM, A0, SPK, CF, LU, ST, STB,
    az_ss, az_rs, ax_ss, ax_rs, r0_ss, r0_rs, re_ss, re_rs, ri_ss, ri_rs, t_ss, t_rs,
    v_s, rb_s, cb_s, cc_s, o_s,
):
    me = lax.axis_index("rad")
    az = lax.axis_index("az")
    ax = lax.axis_index("ax")
    left = lax.rem(az + naz - 1, naz)
    right = lax.rem(az + 1, naz)
    other = 1 - ax
    near, far = 1 - ax, ax
    peers = [lax.rem(me + d, n) for d in range(1, n)]
    GI = (NTL - 4) // 4
    first_of = (2, 2 + 3 * GI, 2 + GI, 2 + 2 * GI)
    edge_first = (0, NTL - 2)
    bf = jnp.bfloat16

    def v_copy(t, j):
        return pltpu.make_async_copy(
            v.at[:, j, pl.ds(128 * t, 128)], F.at[0, t, j, pl.ds(PAD, R), :], v_s.at[t, j])

    def o_copy(t, j):
        return pltpu.make_async_copy(
            F.at[STEPS % 2, t, j, pl.ds(PAD, R), :],
            out.at[:, j, pl.ds(128 * t, 128)], o_s.at[t, j])

    edges = (0, 1, NTL - 2, NTL - 1)
    for j in edges:
        for t in range(2):
            v_copy(t, j).start()
    row_copies = [
        pltpu.make_async_copy(v.at[r], RB0.at[me, pl.ds(q * NTL, NTL), :], rb_s.at[q])
        for q, r in enumerate((0, R - 1))]
    for c in row_copies:
        c.start()
    for j in range(2, NTL - 2):
        for t in range(2):
            v_copy(t, j).start()
    coef_copies = [
        pltpu.make_async_copy(src, STB.at[q], cb_s.at[q]) for q, src in enumerate((rc, ac))]
    for c in coef_copies:
        c.start()

    barrier = pltpu.get_barrier_semaphore()
    for p in peers:
        pl.semaphore_signal(barrier, inc=1, device_id={"rad": p}, device_id_type=MESH)
    for p in (left, right):
        pl.semaphore_signal(barrier, inc=1, device_id={"az": p}, device_id_type=MESH)
    pl.semaphore_signal(barrier, inc=1, device_id={"ax": other}, device_id_type=MESH)
    pl.semaphore_wait(barrier, n + 2)

    def tile_of(p):
        return near if p < 2 else far

    def az_copy(s, p):
        side = p % 2
        return pltpu.make_async_remote_copy(
            src_ref=F.at[lax.rem(s, 2), tile_of(p), pl.ds(edge_first[side], 2), pl.ds(PAD, R), :],
            dst_ref=HA.at[s, p ^ 1], send_sem=az_ss.at[s, p],
            recv_sem=az_rs.at[s, p ^ 1], device_id={"az": (left, right)[side]},
            device_id_type=MESH)

    def ax_copy(s, m):
        return pltpu.make_async_remote_copy(
            src_ref=PS.at[s, m], dst_ref=PR.at[s, m], send_sem=ax_ss.at[s, m],
            recv_sem=ax_rs.at[s, m], device_id={"ax": other}, device_id_type=MESH)

    def rad_send(buf, ss, rs, d):
        return pltpu.make_async_remote_copy(
            src_ref=buf.at[me], dst_ref=buf.at[me], send_sem=ss.at[d],
            recv_sem=rs.at[me], device_id={"rad": peers[d]}, device_id_type=MESH)

    def rad_recv(buf, ss, rs, d):
        return pltpu.make_async_remote_copy(
            src_ref=buf.at[me], dst_ref=buf.at[peers[d]], send_sem=ss.at[d],
            recv_sem=rs.at[peers[d]], device_id={"rad": peers[d]}, device_id_type=MESH)

    for j in edges:
        for t in range(2):
            v_copy(t, j).wait()
    for p in range(4):
        az_copy(0, p).start()
    for c in row_copies:
        c.wait()
    for d in range(n - 1):
        rad_send(RB0, r0_ss, r0_rs, d).start()

    lane = lax.broadcasted_iota(jnp.int32, (CH, 128), 1)

    def members_of(m):
        inner = [first_of[m] + i for i in range(GI)]
        return ([edge_first[m], edge_first[m] + 1] if m < 2 else []) + inner

    def pack(s, m):
        b = lax.rem(s, 2)
        for c in range(R // CH):
            acc = jnp.zeros((CH, 128), F32)
            for i, j in enumerate(members_of(m)):
                edge = F[b, near, j, pl.ds(PAD + c * CH, CH), :]
                acc = jnp.where(lane // 2 == i, pltpu.roll(edge, 2 * i + 2 * (1 - ax), 1), acc)
            PS[s, m, pl.ds(c * CH, CH), :] = acc

    def unpack(s, m):
        for c in range(R // CH):
            rows = pl.ds(c * CH, CH)
            x = PR[s, m, rows, :]
            high = x.astype(bf).astype(F32)
            x = jnp.where(lane < 64, high, pltpu.roll(x - high, 64, 1))
            for i, j in enumerate(members_of(m)):
                FB[j, rows, pl.ds(512, 128)] = jnp.where((lane % 64) // 2 == i, x, 0.0).astype(bf)

    def split_store(j, rows, t, x):
        high = x.astype(bf)
        at = pl.multiple_of(t * 128, 128) if not isinstance(t, int) else t * 128
        FB[j, rows, pl.ds(at, 128)] = high
        FB[j, rows, pl.ds(256 + at, 128)] = (x - high.astype(F32)).astype(bf)

    for j in range(2, NTL - 2):
        for t in range(2):
            v_copy(t, j).wait()

    def first_split(j, carry):
        for t in range(2):
            for c in range(R // CH):
                rows = pl.ds(c * CH, CH)
                split_store(j, rows, t, F[0, t, j, pl.ds(PAD + c * CH, CH), :])
        return carry

    for m in range(4):
        pack(0, m)
        ax_copy(0, m).start()
    lax.fori_loop(0, NTL, first_split, 0)

    row = lax.broadcasted_iota(jnp.int32, (R, 128), 0)
    spacing = 1.0 / (NR + 1)
    radius = 1.0 + ((me * R + row).astype(F32) + 1.0) * spacing
    rdiff = jnp.transpose(jnp.broadcast_to(
        jnp.concatenate([rd[...]] * (128 // R), axis=1), (128, 128)))[0:R, :]
    inward = rdiff * (radius - 0.5 * spacing) / radius
    outward = rdiff * (radius + 0.5 * spacing) / radius
    sink = rdiff * spacing * spacing / (radius * radius)
    grow = 1.0 + sink
    KC[0] = inward
    KC[1] = outward
    KC[2] = grow / outward
    KC[3] = -1.0 / radius
    KC[4] = 1.0 / (radius * radius)
    KC[5] = inward / outward
    KC[6] = grow / inward
    KC[7] = outward / inward
    A0[...] = 66.0 - 30.0 * KC[4]

    lane1 = lax.broadcasted_iota(jnp.int32, (1, 128), 1)
    ones = jnp.ones((1, 128), F32)

    def march(i, carry):
        phi, p, psi, m = carry
        k = R - 1 - i
        PHI[pl.ds(i, 1), :] = phi
        PSI[pl.ds(k, 1), :] = psi
        DM[pl.ds(k, 1), :] = m
        p = KC[2, pl.ds(i, 1), :] * phi + KC[5, pl.ds(i, 1), :] * p
        m = KC[6, pl.ds(k, 1), :] * psi + KC[7, pl.ds(k, 1), :] * m
        DP[pl.ds(i, 1), :] = p
        return phi + p, p, psi + m, m

    lax.fori_loop(0, R, march, (ones, ones, ones, ones))
    weight = 1.0 / (KC[1] * (DP[...] * PSI[...] + PHI[...] * DM[...]))
    at_i = lax.broadcasted_iota(jnp.int32, (R, R), 0)
    at_j = lax.broadcasted_iota(jnp.int32, (R, R), 1)
    upper_part = jnp.transpose(PSI[...] * weight)[0:R, :]
    lower_part = jnp.transpose(PHI[...] * weight)[0:R, :]
    inverse = jnp.where(at_i <= at_j, PHI[:, 0:R] * upper_part, PSI[:, 0:R] * lower_part)
    SPK[0] = -KC[0, 0:1, :] * jnp.broadcast_to(inverse[:, 0:1], (R, 128))
    SPK[1] = -KC[1, R - 1 : R, :] * jnp.broadcast_to(inverse[:, R - 1 : R], (R, 128))
    inverse = inverse * (1.0 / SCALE)
    high = inverse.astype(bf)
    MA[:, 0:R] = high
    MA[:, R : 2 * R] = high
    MB[...] = (inverse - high.astype(F32)).astype(bf)
    TB[me, 0:1, :] = SPK[0, 0:1, :]
    TB[me, 1:2, :] = SPK[1, 0:1, :]
    TB[me, 2:3, :] = SPK[0, R - 1 : R, :]
    TB[me, 3:4, :] = SPK[1, R - 1 : R, :]
    TB[me, 4:8, :] = jnp.zeros((4, 128), F32)
    for d in range(n - 1):
        rad_send(TB, t_ss, t_rs, d).start()

    def band(source, t):
        d = source - (128 * t + lax.broadcasted_iota(jnp.int32, (CH, 128), 1))
        slope = (jnp.where(d == 1, -32.0, 0.0) + jnp.where(d == -1, 32.0, 0.0)
                 + jnp.where(d == 2, 4.0, 0.0) + jnp.where(d == -2, -4.0, 0.0))
        curve = (jnp.where(jnp.abs(d) == 1, 16.0, 0.0) - jnp.where(jnp.abs(d) == 2, 1.0, 0.0))
        return slope.astype(bf), curve.astype(bf)

    here = lax.broadcasted_iota(jnp.int32, (CH, 128), 0)

    def bands(c, carry):
        r0 = pl.multiple_of(c * CH, CH)
        for t in range(2):
            slope, curve = band(here + c * CH, t)
            for q in range(2):
                BW[t, pl.ds(pl.multiple_of(q * 256 + r0, CH), CH), 0:128] = slope
                BW[t, pl.ds(pl.multiple_of(q * 256 + r0, CH), CH), 128:256] = curve
        return carry

    lax.fori_loop(0, 256 // CH, bands, 0)
    for t in range(2):
        slope, curve = band(jnp.where(ax == 0, 256 + here % 2, here % 2 - 2), t)
        for c in range(128 // CH):
            BW[t, pl.ds(512 + c * CH, CH), 0:128] = slope
            BW[t, pl.ds(512 + c * CH, CH), 128:256] = curve

    for q, (dst, scale) in enumerate(((RCF, -0.5 * SCALE), (ACF, None))):
        coef_copies[q].wait()
        moves = []
        for t in range(2):
            def convert(c, carry):
                rows = pl.ds(pl.multiple_of(c * 8, 8), 8)
                x = STB[q, rows, :, pl.ds(128 * t, 128)].astype(F32)
                ST[t, rows] = x if scale is None else x * scale
                return carry

            lax.fori_loop(0, R // 8, convert, 0)
            for j in range(NTL):
                moves.append(pltpu.make_async_copy(ST.at[t, :, j, :], dst.at[t, j], cc_s.at[t, j]))
                moves[-1].start()
        for c in moves:
            c.wait()

    for d in range(n - 1):
        rad_recv(RB0, r0_ss, r0_rs, d).wait_recv()
    below = jnp.maximum(me - 1, 0)
    above = jnp.minimum(me + 1, n - 1)
    low0 = jnp.where(me > 0, RB0[below, NTL : 2 * NTL, :], 0.0)
    high0 = jnp.where(me < n - 1, RB0[above, 0:NTL, :], 0.0)
    for j in range(NTL):
        for t in range(2):
            F[0, t, j, PAD - 1 : PAD, :] = low0[j : j + 1, 128 * t : 128 * t + 128]
            F[0, t, j, PAD + R : PAD + R + 1, :] = high0[j : j + 1, 128 * t : 128 * t + 128]

    for d in range(n - 1):
        rad_recv(TB, t_ss, t_rs, d).wait_recv()
    members = []
    for k in range(n):
        members.append((
            jnp.where(lane1 == 2 * k, 1.0, 0.0),
            jnp.where(lane1 == 2 * k + 1, 1.0, 0.0),
            tuple(TB[k, q : q + 1, :] for q in range(4)),
        ))
    lower_map, upper_map = interface_rows(members, me, n)
    for m in range(2 * n):
        for h, vec in enumerate((lower_map, upper_map)):
            val = jnp.sum(jnp.where(lane1 == m, vec, 0.0), axis=1, keepdims=True)
            CF[h, m // 2, m % 2 : m % 2 + 1, :] = jnp.broadcast_to(val, (1, 128))

    def right_side(b, t, j, r0, near_by, slope, curve):
        rows = pl.ds(PAD + r0, CH)
        at = pl.ds(r0, CH)
        f = F[b, t, j, rows, :]
        lo = F[b, t, j, pl.ds(PAD + r0 - 1, CH), :]
        up = F[b, t, j, pl.ds(PAD + r0 + 1, CH), :]
        m2, m1, p1, p2 = near_by
        dt = 8.0 * (p1 - m1) - (p2 - m2)
        lt = 16.0 * (p1 + m1) - (p2 + m2)
        return (
            f * (A0[at, :] + KC[3, at, :] * dt) + KC[4, at, :] * lt
            + RCF[t, j, at, :] * (up - lo) + (ACF[t, j, at, :] * slope + curve)
        )

    def solve(q):
        return (jnp.dot(MA[...], q[...], preferred_element_type=F32)
                + jnp.dot(MB[...], q[0:R, :], preferred_element_type=F32))

    def put_q(q, r0, cols, x):
        high = x.astype(bf)
        q[pl.ds(r0, CH), cols] = high
        q[pl.ds(R + r0, CH), cols] = (x - high.astype(F32)).astype(bf)

    def axial_edges(side):
        lhs = FB[pl.ds(edge_first[side], 2)].reshape(2 * R, 640)
        for t in range(2):
            SCE[side, t] = jnp.dot(lhs, BW[t], preferred_element_type=F32)

    def edge_solve(s, p):
        side = p % 2
        b = lax.rem(s, 2)
        t = tile_of(p)

        def layer(j, r0):
            if j < 0:
                return HA[s, p, 2 + j, pl.ds(r0, CH), :]
            if j >= NTL:
                return HA[s, p, j - NTL, pl.ds(r0, CH), :]
            return F[b, t, j, pl.ds(PAD + r0, CH), :]

        az_copy(s, p ^ 1).wait_recv()
        for i in range(2):
            j = edge_first[side] + i
            for c in range(R // CH):
                r0 = c * CH
                at = pl.ds(i * R + r0, CH)
                x = right_side(
                    b, t, j, r0, [layer(j + o, r0) for o in (-2, -1, 1, 2)],
                    SCE[side, t, at, 0:128], SCE[side, t, at, 128:256])
                put_q(QE, r0, pl.ds(i * 128, 128), x)
        y = solve(QE)
        YE[p] = y
        RBE[s, p, me, 0:1, :] = y[0:1, :]
        RBE[s, p, me, 1:2, :] = y[R - 1 : R, :]
        for d in range(n - 1):
            rad_send(RBE.at[s, p], re_ss.at[s, p], re_rs.at[s, p], d).start()

    def ends(buf, idx, width):
        res = []
        for h in range(2):
            total = None
            for k in range(n):
                coef = jnp.concatenate([CF[h, k]] * (width // 128), axis=1)
                term = coef * buf[(*idx, k)]
                total = term if total is None else total + term
            res.append(total[0:1, :] + total[1:2, :])
        return res

    def advance(b, t, j, y_of, low, high):
        for c in range(R // CH):
            here = pl.ds(c * CH, CH)
            rows = pl.ds(PAD + c * CH, CH)
            x = (y_of(here) - SPK[0, here, :] * low - SPK[1, here, :] * high - F[b, t, j, rows, :])
            F[1 - b, t, j, rows, :] = x
            split_store(j, here, t, x)
        F[1 - b, t, j, PAD - 1 : PAD, :] = low - F[b, t, j, PAD - 1 : PAD, :]
        F[1 - b, t, j, PAD + R : PAD + R + 1, :] = high - F[b, t, j, PAD + R : PAD + R + 1, :]

    def edge_finish(s, p):
        b = lax.rem(s, 2)
        t = tile_of(p)
        buf, ss, rs = RBE.at[s, p], re_ss.at[s, p], re_rs.at[s, p]
        az_copy(s, p).wait_send()
        for d in range(n - 1):
            rad_send(buf, ss, rs, d).wait_send()
        for d in range(n - 1):
            rad_recv(buf, ss, rs, d).wait_recv()
        low, high = ends(RBE, (s, p), 256)
        for i in range(2):
            cols = slice(i * 128, i * 128 + 128)
            advance(b, t, edge_first[p % 2] + i,
                    lambda here: YE[p, here, cols], low[:, cols], high[:, cols])

        @pl.when(s < STEPS - 1)
        def _():
            az_copy(s + 1, p).start()

        if p >= 2:
            @pl.when(s == STEPS - 1)
            def _():
                for i in range(2):
                    for tt in range(2):
                        o_copy(tt, edge_first[p % 2] + i).start()

    def inner_solve(s, k):
        b = lax.rem(s, 2)
        lhs = FB[pl.ds(first_of[k], GI)].reshape(GI * R, 640)
        for t in range(2):
            SC[t] = jnp.dot(lhs, BW[t], preferred_element_type=F32)

        def rhs(i):
            j = first_of[k] + i
            for t in range(2):
                for c in range(R // CH):
                    r0 = c * CH
                    at = pl.ds(pl.multiple_of(i * R + r0, CH), CH)
                    x = right_side(
                        b, t, j, r0,
                        [F[b, t, j + o, pl.ds(PAD + r0, CH), :] for o in (-2, -1, 1, 2)],
                        SC[t, at, 0:128], SC[t, at, 128:256])
                    put_q(Q.at[i], r0, pl.ds(t * 128, 128), x)

        def close(i):
            y = solve(Q.at[i])
            Y[k, i] = y
            cols = pl.ds(pl.multiple_of(i * NZL, NZL), NZL)
            RBI[s, k, me, 0:1, cols] = y[0:1, :]
            RBI[s, k, me, 1:2, cols] = y[R - 1 : R, :]

        rhs(0)

        def body(i, c):
            close(i - 1)
            rhs(i)
            return c

        lax.fori_loop(1, GI, body, 0)
        close(GI - 1)
        for d in range(n - 1):
            rad_send(RBI.at[s, k], ri_ss.at[s, k], ri_rs.at[s, k], d).start()

    def inner_finish(s, k):
        b = lax.rem(s, 2)
        buf, ss, rs = RBI.at[s, k], ri_ss.at[s, k], ri_rs.at[s, k]
        for d in range(n - 1):
            rad_send(buf, ss, rs, d).wait_send()
        for d in range(n - 1):
            rad_recv(buf, ss, rs, d).wait_recv()
        for h, line in enumerate(ends(RBI, (s, k), GI * NZL)):
            LU[h : h + 1, :] = line

        def body(i, c):
            for t in range(2):
                cols = pl.ds(pl.multiple_of(i * NZL + t * 128, 128), 128)
                advance(b, t, first_of[k] + i,
                        lambda here: Y[k, i, here, pl.ds(t * 128, 128)],
                        LU[0:1, cols], LU[1:2, cols])
            return c

        lax.fori_loop(0, GI, body, 0)

        @pl.when(s < STEPS - 1)
        def _():
            pack(s + 1, k)
            ax_copy(s + 1, k).start()

        @pl.when(s == STEPS - 1)
        def _():
            for i in range(GI):
                for t in range(2):
                    o_copy(t, first_of[k] + i).start()

    def step(s, carry):
        for k in range(4):
            ax_copy(s, k).wait_recv()
            unpack(s, k)
            if k < 2:
                axial_edges(k)
            edge_solve(s, k)
            if k < 2:
                @pl.when(s > 0)
                def _():
                    inner_finish(s - 1, k + 2)
            else:
                inner_finish(s, k - 2)
            if k == 0:
                @pl.when(s > 0)
                def _():
                    edge_finish(s - 1, 3)
            else:
                edge_finish(s, k - 1)
            inner_solve(s, k)
            ax_copy(s, k).wait_send()
        return carry

    lax.fori_loop(0, STEPS, step, 0)
    inner_finish(STEPS - 1, 2)
    edge_finish(STEPS - 1, 3)
    inner_finish(STEPS - 1, 3)
    for j in range(NTL):
        for t in range(2):
            o_copy(t, j).wait()
    for d in range(n - 1):
        rad_send(RB0, r0_ss, r0_rs, d).wait_send()
        rad_send(TB, t_ss, t_rs, d).wait_send()


def local(n, naz, velocity, radial_courant, axial_courant, radial_diffusion):
    R, NTL, NZL = velocity.shape
    S = STEPS
    GI = (NTL - 4) // 4
    dma = pltpu.SemaphoreType.DMA
    bf = jnp.bfloat16
    hbm = pl.BlockSpec(memory_space=pl.ANY)
    return pl.pallas_call(
        functools.partial(kernel, n, naz, R, NTL, NZL),
        out_shape=jax.ShapeDtypeStruct((R, NTL, NZL), F32),
        in_specs=[hbm, hbm, hbm, pl.BlockSpec(memory_space=pltpu.VMEM)],
        out_specs=hbm,
        scratch_shapes=[
            pltpu.VMEM((2, 2, NTL, R + 2 * PAD, 128), F32),
            pltpu.VMEM((NTL, R, 640), bf),
            pltpu.VMEM((S, 4, 2, R, 128), F32),
            pltpu.VMEM((4, GI, R, NZL), F32),
            pltpu.VMEM((4, R, 256), F32),
            pltpu.VMEM((GI, 2 * R, NZL), bf),
            pltpu.VMEM((2 * R, 256), bf),
            pltpu.VMEM((2, GI * R, 256), F32),
            pltpu.VMEM((2, 2, 2 * R, 256), F32),
            pltpu.VMEM((2, NTL, R, 128), F32),
            pltpu.VMEM((2, NTL, R, 128), F32),
            pltpu.VMEM((2, 640, 256), bf),
            pltpu.VMEM((S, 4, R, 128), F32),
            pltpu.VMEM((S, 4, R, 128), F32),
            pltpu.VMEM((n, 2 * NTL, NZL), F32),
            pltpu.VMEM((S, 4, n, 2, 256), F32),
            pltpu.VMEM((S, 4, n, 2, GI * NZL), F32),
            pltpu.VMEM((n, 8, 128), F32),
            pltpu.VMEM((R, 2 * R), bf),
            pltpu.VMEM((R, R), bf),
            pltpu.VMEM((8, R, 128), F32),
            pltpu.VMEM((R, 128), F32),
            pltpu.VMEM((R, 128), F32),
            pltpu.VMEM((R, 128), F32),
            pltpu.VMEM((R, 128), F32),
            pltpu.VMEM((R, 128), F32),
            pltpu.VMEM((2, R, 128), F32),
            pltpu.VMEM((2, n, 2, 128), F32),
            pltpu.VMEM((2, GI * NZL), F32),
            pltpu.VMEM((2, R, NTL, 128), F32),
            pltpu.VMEM((2, R, NTL, NZL), bf),
            dma((S, 4)), dma((S, 4)), dma((S, 4)), dma((S, 4)),
            dma((n,)), dma((n,)), dma((S, 4, n)), dma((S, 4, n)),
            dma((S, 4, n)), dma((S, 4, n)), dma((n,)), dma((n,)),
            dma((2, NTL)), dma((2,)), dma((2,)), dma((2, NTL)), dma((2, NTL)),
        ],
        compiler_params=pltpu.CompilerParams(
            collective_id=0, has_side_effects=True, vmem_limit_bytes=58 * 1024 * 1024),
    )(velocity, radial_courant, axial_courant, radial_diffusion.reshape(1, R))


def solution(mesh):
    return jax.shard_map(
        functools.partial(local, mesh.shape["rad"], mesh.shape["az"]),
        mesh=mesh,
        in_specs=(P("rad", "az", "ax"), P("rad", "az", "ax"), P("rad", "az", "ax"), P("rad")),
        out_specs=P("rad", "az", "ax"),
        check_vma=False,
    )
```

```python
import functools

import jax
import jax.numpy as jnp
from jax import lax
from jax.experimental import pallas as pl
from jax.experimental.pallas import tpu as pltpu
from jax.sharding import PartitionSpec as P

NR = 512
STEPS = 6
F32 = jnp.float32
MESH = pl.DeviceIdType.MESH
PAD = 8
CH = 16


def join_slabs(left, right):
    head_l, tail_l, tl = left
    head_r, tail_r, tr = right
    divisor = 1.0 - tl[3] * tr[0]
    mid_value = (tail_l - tl[3] * head_r) / divisor
    mid_left = tl[2] / divisor
    mid_right = -tl[3] * tr[1] / divisor
    next_value = head_r - tr[0] * mid_value
    next_left = -tr[0] * mid_left
    next_right = tr[1] - tr[0] * mid_right
    return (
        head_l - tl[1] * next_value,
        tail_r - tr[2] * mid_value,
        (
            tl[0] - tl[1] * next_left,
            -tl[1] * next_right,
            -tr[2] * mid_left,
            tr[3] - tr[2] * mid_right,
        ),
    )


def interface_rows(members, me, n):
    zero = jnp.zeros_like(members[0][0])
    identity = (zero, zero, (zero, zero - 1.0, zero - 1.0, zero))

    def choose(cond, a, b):
        return jax.tree.map(lambda x, y: jnp.where(cond, x, y), a, b)

    prefix = identity
    own = members[0]
    for k in range(n):
        own = choose(k == me, members[k], own)
        prefix = choose(k < me, join_slabs(prefix, members[k]), prefix)
    suffix = identity
    for k in range(n - 1, -1, -1):
        suffix = choose(k > me, join_slabs(members[k], suffix), suffix)
    combined = join_slabs(own, suffix)
    lower = (prefix[1] - prefix[2][3] * combined[0]) / (1.0 - prefix[2][3] * combined[2][0])
    upper = (suffix[0] - suffix[2][0] * (own[1] - own[2][2] * lower)) / (
        1.0 - suffix[2][0] * own[2][3]
    )
    return lower, upper


SCALE = 48.0


def kernel(
    n, naz, R, NTL, NZL,
    v, rc, ac, rd, out,
    F, FB, HA, HX, LS, LR, Y, YE, Q, QE, SC, SCE, RCF, ACF, BW, PS, PR, RB0, RBE, RBI, TB, MA, MB, KC,
    PHI, PSI, DP, DM, A0, SPK, CF, LU, ST, STB,
    a0_ss, a0_rs, az_ss, az_rs, lh_ss, lh_rs, ax_ss, ax_rs, r0_ss, r0_rs, re_ss, re_rs, ri_ss, ri_rs, t_ss, t_rs,
    v_s, rb_s, cb_s, cc_s, o_s,
):
    me = lax.axis_index("rad")
    az = lax.axis_index("az")
    ax = lax.axis_index("ax")
    left = lax.rem(az + naz - 1, naz)
    right = lax.rem(az + 1, naz)
    other = 1 - ax
    near, far = 1 - ax, ax
    peers = [lax.rem(me + d, n) for d in range(1, n)]
    GI = (NTL - 4) // 4
    first_of = (2, 2 + 3 * GI, 2 + GI, 2 + 2 * GI)
    edge_first = (0, NTL - 2)
    bf = jnp.bfloat16

    def v_copy(t, j):
        return pltpu.make_async_copy(
            v.at[:, j, pl.ds(128 * t, 128)], F.at[0, t, j, pl.ds(PAD, R), :], v_s.at[t, j])

    def o_copy(t, j):
        return pltpu.make_async_copy(
            F.at[STEPS % 2, t, j, pl.ds(PAD, R), :],
            out.at[:, j, pl.ds(pl.multiple_of(128 * t, 128), 128)], o_s.at[t, j])

    edges = (0, 1, NTL - 2, NTL - 1)
    for j in edges:
        for t in range(2):
            v_copy(t, j).start()
    row_copies = [
        pltpu.make_async_copy(v.at[r], RB0.at[me, pl.ds(q * NTL, NTL), :], rb_s.at[q])
        for q, r in enumerate((0, R - 1))]
    for c in row_copies:
        c.start()
    for j in range(2, NTL - 2):
        for t in range(2):
            v_copy(t, j).start()
    coef_copies = [
        pltpu.make_async_copy(src, STB.at[q], cb_s.at[q]) for q, src in enumerate((rc, ac))]
    for c in coef_copies:
        c.start()

    barrier = pltpu.get_barrier_semaphore()
    for p in peers:
        pl.semaphore_signal(barrier, inc=1, device_id={"rad": p}, device_id_type=MESH)
    for p in (left, right):
        pl.semaphore_signal(barrier, inc=1, device_id={"az": p}, device_id_type=MESH)
    pl.semaphore_signal(barrier, inc=1, device_id={"ax": other}, device_id_type=MESH)
    pl.semaphore_wait(barrier, n + 2)

    def tile_of(p):
        return near if p < 2 else far

    def az_first(p):
        side = p % 2
        return pltpu.make_async_remote_copy(
            src_ref=F.at[0, tile_of(p), pl.ds(edge_first[side], 2), pl.ds(PAD, R), :],
            dst_ref=HX.at[p ^ 1], send_sem=a0_ss.at[p],
            recv_sem=a0_rs.at[p ^ 1], device_id={"az": (left, right)[side]},
            device_id_type=MESH)

    def az_copy(s, p):
        return pltpu.make_async_remote_copy(
            src_ref=YE.at[s - 1, p], dst_ref=HA.at[s - 1, p ^ 1], send_sem=az_ss.at[s - 1, p],
            recv_sem=az_rs.at[s - 1, p ^ 1], device_id={"az": (left, right)[p % 2]},
            device_id_type=MESH)

    def lh_copy(s, p):
        return pltpu.make_async_remote_copy(
            src_ref=LS.at[s - 1, p], dst_ref=LR.at[s - 1, p ^ 1], send_sem=lh_ss.at[s - 1, p],
            recv_sem=lh_rs.at[s - 1, p ^ 1], device_id={"az": (left, right)[p % 2]},
            device_id_type=MESH)

    def ax_copy(s, m):
        return pltpu.make_async_remote_copy(
            src_ref=PS.at[s, m], dst_ref=PR.at[s, m], send_sem=ax_ss.at[s, m],
            recv_sem=ax_rs.at[s, m], device_id={"ax": other}, device_id_type=MESH)

    def rad_send(buf, ss, rs, d):
        return pltpu.make_async_remote_copy(
            src_ref=buf.at[me], dst_ref=buf.at[me], send_sem=ss.at[d],
            recv_sem=rs.at[me], device_id={"rad": peers[d]}, device_id_type=MESH)

    def rad_recv(buf, ss, rs, d):
        return pltpu.make_async_remote_copy(
            src_ref=buf.at[me], dst_ref=buf.at[peers[d]], send_sem=ss.at[d],
            recv_sem=rs.at[peers[d]], device_id={"rad": peers[d]}, device_id_type=MESH)

    for j in edges:
        for t in range(2):
            v_copy(t, j).wait()
    for p in range(2):
        az_first(p).start()
    for c in row_copies:
        c.wait()
    for d in range(n - 1):
        rad_send(RB0, r0_ss, r0_rs, d).start()

    lane = lax.broadcasted_iota(jnp.int32, (CH, 128), 1)

    def members_of(m):
        inner = [first_of[m] + i for i in range(GI)]
        return ([edge_first[m], edge_first[m] + 1] if m < 2 else []) + inner

    def pack(s, m):
        b = lax.rem(s, 2)
        for c in range(R // CH):
            acc = jnp.zeros((CH, 128), F32)
            for i, j in enumerate(members_of(m)):
                edge = F[b, near, j, pl.ds(PAD + c * CH, CH), :]
                acc = jnp.where(lane // 2 == i, pltpu.roll(edge, 2 * i + 2 * (1 - ax), 1), acc)
            PS[s, m, pl.ds(c * CH, CH), :] = acc

    def unpack(s, m):
        for c in range(R // CH):
            rows = pl.ds(c * CH, CH)
            x = PR[s, m, rows, :]
            high = x.astype(bf).astype(F32)
            x = jnp.where(lane < 64, high, pltpu.roll(x - high, 64, 1))
            for i, j in enumerate(members_of(m)):
                FB[j, rows, pl.ds(512, 128)] = jnp.where((lane % 64) // 2 == i, x, 0.0).astype(bf)

    def split_store(j, rows, t, x):
        high = x.astype(bf)
        at = pl.multiple_of(t * 128, 128) if not isinstance(t, int) else t * 128
        FB[j, rows, pl.ds(at, 128)] = high
        FB[j, rows, pl.ds(256 + at, 128)] = (x - high.astype(F32)).astype(bf)

    for j in range(2, NTL - 2):
        for t in range(2):
            v_copy(t, j).wait()

    def first_split(j, carry):
        for t in range(2):
            for c in range(R // CH):
                rows = pl.ds(c * CH, CH)
                split_store(j, rows, t, F[0, t, j, pl.ds(PAD + c * CH, CH), :])
        return carry

    for m in range(4):
        pack(0, m)
        ax_copy(0, m).start()
    lax.fori_loop(0, NTL, first_split, 0)
    for p in range(2, 4):
        az_first(p).start()

    row = lax.broadcasted_iota(jnp.int32, (R, 128), 0)
    spacing = 1.0 / (NR + 1)
    radius = 1.0 + ((me * R + row).astype(F32) + 1.0) * spacing
    rdiff = jnp.transpose(jnp.broadcast_to(
        jnp.concatenate([rd[...]] * (128 // R), axis=1), (128, 128)))[0:R, :]
    inward = rdiff * (radius - 0.5 * spacing) / radius
    outward = rdiff * (radius + 0.5 * spacing) / radius
    sink = rdiff * spacing * spacing / (radius * radius)
    grow = 1.0 + sink
    KC[0] = inward
    KC[1] = outward
    KC[2] = grow / outward
    KC[3] = -1.0 / radius
    KC[4] = 1.0 / (radius * radius)
    KC[5] = inward / outward
    KC[6] = grow / inward
    KC[7] = outward / inward
    A0[...] = 66.0 - 30.0 * KC[4]

    lane1 = lax.broadcasted_iota(jnp.int32, (1, 128), 1)
    ones = jnp.ones((1, 128), F32)

    def march(i, carry):
        phi, p, psi, m = carry
        k = R - 1 - i
        PHI[pl.ds(i, 1), :] = phi
        PSI[pl.ds(k, 1), :] = psi
        DM[pl.ds(k, 1), :] = m
        p = KC[2, pl.ds(i, 1), :] * phi + KC[5, pl.ds(i, 1), :] * p
        m = KC[6, pl.ds(k, 1), :] * psi + KC[7, pl.ds(k, 1), :] * m
        DP[pl.ds(i, 1), :] = p
        return phi + p, p, psi + m, m

    lax.fori_loop(0, R, march, (ones, ones, ones, ones))
    weight = 1.0 / (KC[1] * (DP[...] * PSI[...] + PHI[...] * DM[...]))
    at_i = lax.broadcasted_iota(jnp.int32, (R, R), 0)
    at_j = lax.broadcasted_iota(jnp.int32, (R, R), 1)
    upper_part = jnp.transpose(PSI[...] * weight)[0:R, :]
    lower_part = jnp.transpose(PHI[...] * weight)[0:R, :]
    inverse = jnp.where(at_i <= at_j, PHI[:, 0:R] * upper_part, PSI[:, 0:R] * lower_part)
    SPK[0] = -KC[0, 0:1, :] * jnp.broadcast_to(inverse[:, 0:1], (R, 128))
    SPK[1] = -KC[1, R - 1 : R, :] * jnp.broadcast_to(inverse[:, R - 1 : R], (R, 128))
    inverse = inverse * (1.0 / SCALE)
    high = inverse.astype(bf)
    MA[:, 0:R] = high
    MA[:, R : 2 * R] = high
    MB[...] = (inverse - high.astype(F32)).astype(bf)
    TB[me, 0:1, :] = SPK[0, 0:1, :]
    TB[me, 1:2, :] = SPK[1, 0:1, :]
    TB[me, 2:3, :] = SPK[0, R - 1 : R, :]
    TB[me, 3:4, :] = SPK[1, R - 1 : R, :]
    TB[me, 4:8, :] = jnp.zeros((4, 128), F32)
    for d in range(n - 1):
        rad_send(TB, t_ss, t_rs, d).start()

    def band(source, t):
        d = source - (128 * t + lax.broadcasted_iota(jnp.int32, (CH, 128), 1))
        slope = (jnp.where(d == 1, -32.0, 0.0) + jnp.where(d == -1, 32.0, 0.0)
                 + jnp.where(d == 2, 4.0, 0.0) + jnp.where(d == -2, -4.0, 0.0))
        curve = (jnp.where(jnp.abs(d) == 1, 16.0, 0.0) - jnp.where(jnp.abs(d) == 2, 1.0, 0.0))
        return slope.astype(bf), curve.astype(bf)

    here = lax.broadcasted_iota(jnp.int32, (CH, 128), 0)

    def bands(c, carry):
        r0 = pl.multiple_of(c * CH, CH)
        for t in range(2):
            slope, curve = band(here + c * CH, t)
            for q in range(2):
                BW[t, pl.ds(pl.multiple_of(q * 256 + r0, CH), CH), 0:128] = slope
                BW[t, pl.ds(pl.multiple_of(q * 256 + r0, CH), CH), 128:256] = curve
        return carry

    lax.fori_loop(0, 256 // CH, bands, 0)
    for t in range(2):
        slope, curve = band(jnp.where(ax == 0, 256 + here % 2, here % 2 - 2), t)
        for c in range(128 // CH):
            BW[t, pl.ds(512 + c * CH, CH), 0:128] = slope
            BW[t, pl.ds(512 + c * CH, CH), 128:256] = curve

    for q, (dst, scale) in enumerate(((RCF, -0.5 * SCALE), (ACF, None))):
        coef_copies[q].wait()
        moves = []
        for t in range(2):
            def convert(c, carry):
                rows = pl.ds(pl.multiple_of(c * 8, 8), 8)
                x = STB[q, rows, :, pl.ds(128 * t, 128)].astype(F32)
                ST[t, rows] = x if scale is None else x * scale
                return carry

            lax.fori_loop(0, R // 8, convert, 0)
            for j in range(NTL):
                moves.append(pltpu.make_async_copy(ST.at[t, :, j, :], dst.at[t, j], cc_s.at[t, j]))
                moves[-1].start()
        for c in moves:
            c.wait()

    for d in range(n - 1):
        rad_recv(RB0, r0_ss, r0_rs, d).wait_recv()
    below = jnp.maximum(me - 1, 0)
    above = jnp.minimum(me + 1, n - 1)
    low0 = jnp.where(me > 0, RB0[below, NTL : 2 * NTL, :], 0.0)
    high0 = jnp.where(me < n - 1, RB0[above, 0:NTL, :], 0.0)
    for j in range(NTL):
        for t in range(2):
            F[0, t, j, PAD - 1 : PAD, :] = low0[j : j + 1, 128 * t : 128 * t + 128]
            F[0, t, j, PAD + R : PAD + R + 1, :] = high0[j : j + 1, 128 * t : 128 * t + 128]

    for d in range(n - 1):
        rad_recv(TB, t_ss, t_rs, d).wait_recv()
    members = []
    for k in range(n):
        members.append((
            jnp.where(lane1 == 2 * k, 1.0, 0.0),
            jnp.where(lane1 == 2 * k + 1, 1.0, 0.0),
            tuple(TB[k, q : q + 1, :] for q in range(4)),
        ))
    lower_map, upper_map = interface_rows(members, me, n)
    for m in range(2 * n):
        for h, vec in enumerate((lower_map, upper_map)):
            val = jnp.sum(jnp.where(lane1 == m, vec, 0.0), axis=1, keepdims=True)
            CF[h, m // 2, m % 2 : m % 2 + 1, :] = jnp.broadcast_to(val, (1, 128))

    def right_side(b, t, j, r0, near_by, slope, curve):
        rows = pl.ds(PAD + r0, CH)
        at = pl.ds(r0, CH)
        f = F[b, t, j, rows, :]
        lo = F[b, t, j, pl.ds(PAD + r0 - 1, CH), :]
        up = F[b, t, j, pl.ds(PAD + r0 + 1, CH), :]
        m2, m1, p1, p2 = near_by
        dt = 8.0 * (p1 - m1) - (p2 - m2)
        lt = 16.0 * (p1 + m1) - (p2 + m2)
        return (
            f * (A0[at, :] + KC[3, at, :] * dt) + KC[4, at, :] * lt
            + RCF[t, j, at, :] * (up - lo) + (ACF[t, j, at, :] * slope + curve)
        )

    def solve(q):
        return (jnp.dot(MA[...], q[...], preferred_element_type=F32)
                + jnp.dot(MB[...], q[0:R, :], preferred_element_type=F32))

    def put_q(q, r0, cols, x):
        high = x.astype(bf)
        q[pl.ds(r0, CH), cols] = high
        q[pl.ds(R + r0, CH), cols] = (x - high.astype(F32)).astype(bf)

    def axial_edges(side):
        lhs = FB[pl.ds(edge_first[side], 2)].reshape(2 * R, 640)
        for t in range(2):
            SCE[side, t] = jnp.dot(lhs, BW[t], preferred_element_type=F32)

    def edge_solve(s, p):
        side = p % 2
        b = lax.rem(s, 2)
        t = tile_of(p)

        def layer(j, r0):
            if j < 0:
                return HX[p, 2 + j, pl.ds(r0, CH), :]
            if j >= NTL:
                return HX[p, j - NTL, pl.ds(r0, CH), :]
            return F[b, t, j, pl.ds(PAD + r0, CH), :]

        @pl.when(s == 0)
        def _():
            az_first(p ^ 1).wait_recv()
            az_first(p).wait_send()

        @pl.when(s > 0)
        def _():
            for copy in (az_copy, lh_copy):
                copy(s, p ^ 1).wait_recv()
                copy(s, p).wait_send()
            for i in range(2):
                cols = slice(i * 128, i * 128 + 128)
                low = LR[s - 1, p, 0:1, cols]
                high = LR[s - 1, p, 1:2, cols]
                for c in range(R // CH):
                    here = pl.ds(c * CH, CH)
                    HX[p, i, here, :] = (
                        HA[s - 1, p, here, cols] - SPK[0, here, :] * low
                        - SPK[1, here, :] * high - HX[p, i, here, :])

        for i in range(2):
            j = edge_first[side] + i
            for c in range(R // CH):
                r0 = c * CH
                at = pl.ds(i * R + r0, CH)
                x = right_side(
                    b, t, j, r0, [layer(j + o, r0) for o in (-2, -1, 1, 2)],
                    SCE[side, t, at, 0:128], SCE[side, t, at, 128:256])
                put_q(QE, r0, pl.ds(i * 128, 128), x)
        y = solve(QE)
        YE[s, p] = y
        RBE[s, p, me, 0:1, :] = y[0:1, :]
        RBE[s, p, me, 1:2, :] = y[R - 1 : R, :]
        for d in range(n - 1):
            rad_send(RBE.at[s, p], re_ss.at[s, p], re_rs.at[s, p], d).start()

        @pl.when(s < STEPS - 1)
        def _():
            az_copy(s + 1, p).start()

    def ends(buf, idx, width):
        res = []
        for h in range(2):
            total = None
            for k in range(n):
                coef = jnp.concatenate([CF[h, k]] * (width // 128), axis=1)
                term = coef * buf[(*idx, k)]
                total = term if total is None else total + term
            res.append(total[0:1, :] + total[1:2, :])
        return res

    def advance(b, t, j, y_of, low, high):
        for c in range(R // CH):
            here = pl.ds(c * CH, CH)
            rows = pl.ds(PAD + c * CH, CH)
            x = (y_of(here) - SPK[0, here, :] * low - SPK[1, here, :] * high - F[b, t, j, rows, :])
            F[1 - b, t, j, rows, :] = x
            split_store(j, here, t, x)
        F[1 - b, t, j, PAD - 1 : PAD, :] = low - F[b, t, j, PAD - 1 : PAD, :]
        F[1 - b, t, j, PAD + R : PAD + R + 1, :] = high - F[b, t, j, PAD + R : PAD + R + 1, :]

    def edge_finish(s, p):
        b = lax.rem(s, 2)
        t = tile_of(p)
        buf, ss, rs = RBE.at[s, p], re_ss.at[s, p], re_rs.at[s, p]
        for d in range(n - 1):
            rad_send(buf, ss, rs, d).wait_send()
        for d in range(n - 1):
            rad_recv(buf, ss, rs, d).wait_recv()
        low, high = ends(RBE, (s, p), 256)

        @pl.when(s < STEPS - 1)
        def _():
            LS[s, p, 0:1, :] = low
            LS[s, p, 1:2, :] = high
            lh_copy(s + 1, p).start()

        for i in range(2):
            cols = slice(i * 128, i * 128 + 128)
            advance(b, t, edge_first[p % 2] + i,
                    lambda here: YE[s, p, here, cols], low[:, cols], high[:, cols])

        @pl.when(s == STEPS - 1)
        def _():
            for i in range(2):
                o_copy(t, edge_first[p % 2] + i).start()

    def inner_solve(s, k):
        b = lax.rem(s, 2)
        lhs = FB[pl.ds(first_of[k], GI)].reshape(GI * R, 640)
        for t in range(2):
            SC[t] = jnp.dot(lhs, BW[t], preferred_element_type=F32)

        def rhs(i):
            j = first_of[k] + i
            for t in range(2):
                for c in range(R // CH):
                    r0 = c * CH
                    at = pl.ds(pl.multiple_of(i * R + r0, CH), CH)
                    x = right_side(
                        b, t, j, r0,
                        [F[b, t, j + o, pl.ds(PAD + r0, CH), :] for o in (-2, -1, 1, 2)],
                        SC[t, at, 0:128], SC[t, at, 128:256])
                    put_q(Q.at[i], r0, pl.ds(t * 128, 128), x)

        def close(i):
            y = solve(Q.at[i])
            Y[k, i] = y
            cols = pl.ds(pl.multiple_of(i * NZL, NZL), NZL)
            RBI[s, k, me, 0:1, cols] = y[0:1, :]
            RBI[s, k, me, 1:2, cols] = y[R - 1 : R, :]

        rhs(0)

        def body(i, c):
            close(i - 1)
            rhs(i)
            return c

        lax.fori_loop(1, GI, body, 0)
        close(GI - 1)
        for d in range(n - 1):
            rad_send(RBI.at[s, k], ri_ss.at[s, k], ri_rs.at[s, k], d).start()

    def inner_finish(s, k):
        b = lax.rem(s, 2)
        buf, ss, rs = RBI.at[s, k], ri_ss.at[s, k], ri_rs.at[s, k]
        for d in range(n - 1):
            rad_send(buf, ss, rs, d).wait_send()
        for d in range(n - 1):
            rad_recv(buf, ss, rs, d).wait_recv()
        for h, line in enumerate(ends(RBI, (s, k), GI * NZL)):
            LU[h : h + 1, :] = line

        def body(i, c):
            for t in range(2):
                cols = pl.ds(pl.multiple_of(i * NZL + t * 128, 128), 128)
                advance(b, t, first_of[k] + i,
                        lambda here: Y[k, i, here, pl.ds(t * 128, 128)],
                        LU[0:1, cols], LU[1:2, cols])
            return c

        lax.fori_loop(0, GI, body, 0)

        @pl.when(s < STEPS - 1)
        def _():
            pack(s + 1, k)
            ax_copy(s + 1, k).start()

        @pl.when(s == STEPS - 1)
        def _():
            for i in range(GI):
                for t in range(2):
                    o_copy(t, first_of[k] + i).start()

    def step(s, carry):
        for k in range(4):
            ax_copy(s, k).wait_recv()
            unpack(s, k)
            inner_solve(s, k)
            if k < 2:
                axial_edges(k)
            edge_solve(s, k)
            if k == 0:
                @pl.when(s > 0)
                def _():
                    edge_finish(s - 1, 3)
                    inner_finish(s - 1, 3)
            else:
                edge_finish(s, k - 1)
                inner_finish(s, k - 1)
            ax_copy(s, k).wait_send()
        return carry

    lax.fori_loop(0, STEPS, step, 0)
    inner_finish(STEPS - 1, 3)
    edge_finish(STEPS - 1, 3)
    for j in range(NTL):
        for t in range(2):
            o_copy(t, j).wait()
    for d in range(n - 1):
        rad_send(RB0, r0_ss, r0_rs, d).wait_send()
        rad_send(TB, t_ss, t_rs, d).wait_send()


def local(n, naz, velocity, radial_courant, axial_courant, radial_diffusion):
    R, NTL, NZL = velocity.shape
    S = STEPS
    GI = (NTL - 4) // 4
    dma = pltpu.SemaphoreType.DMA
    bf = jnp.bfloat16
    hbm = pl.BlockSpec(memory_space=pl.ANY)
    return pl.pallas_call(
        functools.partial(kernel, n, naz, R, NTL, NZL),
        out_shape=jax.ShapeDtypeStruct((R, NTL, NZL), F32),
        in_specs=[hbm, hbm, hbm, pl.BlockSpec(memory_space=pltpu.VMEM)],
        out_specs=hbm,
        scratch_shapes=[
            pltpu.VMEM((2, 2, NTL, R + 2 * PAD, 128), F32),
            pltpu.VMEM((NTL, R, 640), bf),
            pltpu.VMEM((S - 1, 4, R, 256), F32),
            pltpu.VMEM((4, 2, R, 128), F32),
            pltpu.VMEM((S - 1, 4, 2, 256), F32),
            pltpu.VMEM((S - 1, 4, 2, 256), F32),
            pltpu.VMEM((4, GI, R, NZL), F32),
            pltpu.VMEM((S, 4, R, 256), F32),
            pltpu.VMEM((GI, 2 * R, NZL), bf),
            pltpu.VMEM((2 * R, 256), bf),
            pltpu.VMEM((2, GI * R, 256), F32),
            pltpu.VMEM((2, 2, 2 * R, 256), F32),
            pltpu.VMEM((2, NTL, R, 128), F32),
            pltpu.VMEM((2, NTL, R, 128), F32),
            pltpu.VMEM((2, 640, 256), bf),
            pltpu.VMEM((S, 4, R, 128), F32),
            pltpu.VMEM((S, 4, R, 128), F32),
            pltpu.VMEM((n, 2 * NTL, NZL), F32),
            pltpu.VMEM((S, 4, n, 2, 256), F32),
            pltpu.VMEM((S, 4, n, 2, GI * NZL), F32),
            pltpu.VMEM((n, 8, 128), F32),
            pltpu.VMEM((R, 2 * R), bf),
            pltpu.VMEM((R, R), bf),
            pltpu.VMEM((8, R, 128), F32),
            pltpu.VMEM((R, 128), F32),
            pltpu.VMEM((R, 128), F32),
            pltpu.VMEM((R, 128), F32),
            pltpu.VMEM((R, 128), F32),
            pltpu.VMEM((R, 128), F32),
            pltpu.VMEM((2, R, 128), F32),
            pltpu.VMEM((2, n, 2, 128), F32),
            pltpu.VMEM((2, GI * NZL), F32),
            pltpu.VMEM((2, R, NTL, 128), F32),
            pltpu.VMEM((2, R, NTL, NZL), bf),
            dma((4,)), dma((4,)), dma((S - 1, 4)), dma((S - 1, 4)), dma((S - 1, 4)), dma((S - 1, 4)),
            dma((S, 4)), dma((S, 4)),
            dma((n,)), dma((n,)), dma((S, 4, n)), dma((S, 4, n)),
            dma((S, 4, n)), dma((S, 4, n)), dma((n,)), dma((n,)),
            dma((2, NTL)), dma((2,)), dma((2,)), dma((2, NTL)), dma((2, NTL)),
        ],
        compiler_params=pltpu.CompilerParams(
            collective_id=0, has_side_effects=True, vmem_limit_bytes=58 * 1024 * 1024),
    )(velocity, radial_courant, axial_courant, radial_diffusion.reshape(1, R))


def solution(mesh):
    return jax.shard_map(
        functools.partial(local, mesh.shape["rad"], mesh.shape["az"]),
        mesh=mesh,
        in_specs=(P("rad", "az", "ax"), P("rad", "az", "ax"), P("rad", "az", "ax"), P("rad")),
        out_specs=P("rad", "az", "ax"),
        check_vma=False,
    )
```

```python
import functools

import jax
import jax.numpy as jnp
from jax import lax
from jax.experimental import pallas as pl
from jax.experimental.pallas import tpu as pltpu
from jax.sharding import PartitionSpec as P

NR = 512
STEPS = 6
F32 = jnp.float32
MESH = pl.DeviceIdType.MESH
PAD = 8
CH = 16


def join_slabs(left, right):
    head_l, tail_l, tl = left
    head_r, tail_r, tr = right
    divisor = 1.0 - tl[3] * tr[0]
    mid_value = (tail_l - tl[3] * head_r) / divisor
    mid_left = tl[2] / divisor
    mid_right = -tl[3] * tr[1] / divisor
    next_value = head_r - tr[0] * mid_value
    next_left = -tr[0] * mid_left
    next_right = tr[1] - tr[0] * mid_right
    return (
        head_l - tl[1] * next_value,
        tail_r - tr[2] * mid_value,
        (
            tl[0] - tl[1] * next_left,
            -tl[1] * next_right,
            -tr[2] * mid_left,
            tr[3] - tr[2] * mid_right,
        ),
    )


def interface_rows(members, me, n):
    zero = jnp.zeros_like(members[0][0])
    identity = (zero, zero, (zero, zero - 1.0, zero - 1.0, zero))

    def choose(cond, a, b):
        return jax.tree.map(lambda x, y: jnp.where(cond, x, y), a, b)

    prefix = identity
    own = members[0]
    for k in range(n):
        own = choose(k == me, members[k], own)
        prefix = choose(k < me, join_slabs(prefix, members[k]), prefix)
    suffix = identity
    for k in range(n - 1, -1, -1):
        suffix = choose(k > me, join_slabs(members[k], suffix), suffix)
    combined = join_slabs(own, suffix)
    lower = (prefix[1] - prefix[2][3] * combined[0]) / (1.0 - prefix[2][3] * combined[2][0])
    upper = (suffix[0] - suffix[2][0] * (own[1] - own[2][2] * lower)) / (
        1.0 - suffix[2][0] * own[2][3]
    )
    return lower, upper


SCALE = 48.0


def kernel(
    n, naz, R, NTL, NZL,
    v, rc, ac, rd, out,
    F, FB, HA, LS, LR, Y, YE, Q, QE, SC, SCE, RCF, ACF, BW, PS, PR, RB0, RBE, RBI, TB, MA, MB, KC,
    PHI, PSI, DP, DM, A0, SPK, CF, STB,
    a0_ss, a0_rs, az_ss, az_rs, lh_ss, lh_rs, ax_ss, ax_rs, r0_ss, r0_rs, re_ss, re_rs, ri_ss, ri_rs, t_ss, t_rs,
    v_s, rb_s, cb_s, o_s,
):
    me = lax.axis_index("rad")
    az = lax.axis_index("az")
    ax = lax.axis_index("ax")
    left = lax.rem(az + naz - 1, naz)
    right = lax.rem(az + 1, naz)
    other = 1 - ax
    near, far = 1 - ax, ax
    peers = [lax.rem(me + d, n) for d in range(1, n)]
    GI = (NTL - 4) // 4
    parity = lax.rem(az, 2)

    def group(k, q):
        lowest = (2, 2 + 3 * GI, 2 + GI, 2 + 2 * GI)
        return lowest[k] if q == 0 else lowest[k ^ 1]

    def edge(p, q):
        return (NTL - 2) * ((p % 2) ^ q)

    first_of = [group(k, 0) + parity * (group(k, 1) - group(k, 0)) for k in range(4)]
    edge_first = [edge(p, 0) + parity * (edge(p, 1) - edge(p, 0)) for p in range(2)]
    side_of = [p + parity * (1 - 2 * p) for p in range(2)]
    beside = [lax.rem(az + naz - 1 + 2 * side_of[p], naz) for p in range(2)]
    bf = jnp.bfloat16

    def v_copy(t, j):
        return pltpu.make_async_copy(
            v.at[:, j, pl.ds(128 * t, 128)], F.at[0, t, j + 2, pl.ds(PAD, R), :], v_s.at[t, j])

    def o_copy(t, j):
        return pltpu.make_async_copy(
            F.at[STEPS % 2, t, j + 2, pl.ds(PAD, R), :],
            out.at[:, j, pl.ds(pl.multiple_of(128 * t, 128), 128)], o_s.at[t, j])

    edges = (0, 1, NTL - 2, NTL - 1)
    for j in edges:
        for t in range(2):
            v_copy(t, j).start()
    row_copies = [
        pltpu.make_async_copy(v.at[r], RB0.at[me, pl.ds(q * NTL, NTL), :], rb_s.at[q])
        for q, r in enumerate((0, R - 1))]
    for c in row_copies:
        c.start()
    for j in range(2, NTL - 2):
        for t in range(2):
            v_copy(t, j).start()
    coef_copies = [
        pltpu.make_async_copy(src, STB.at[q], cb_s.at[q]) for q, src in enumerate((rc, ac))]
    for c in coef_copies:
        c.start()

    barrier = pltpu.get_barrier_semaphore()
    for p in peers:
        pl.semaphore_signal(barrier, inc=1, device_id={"rad": p}, device_id_type=MESH)
    for p in (left, right):
        pl.semaphore_signal(barrier, inc=1, device_id={"az": p}, device_id_type=MESH)
    pl.semaphore_signal(barrier, inc=1, device_id={"ax": other}, device_id_type=MESH)
    row = lax.broadcasted_iota(jnp.int32, (R, 128), 0)
    spacing = 1.0 / (NR + 1)
    radius = 1.0 + ((me * R + row).astype(F32) + 1.0) * spacing
    rdiff = jnp.transpose(jnp.broadcast_to(
        jnp.concatenate([rd[...]] * (128 // R), axis=1), (128, 128)))[0:R, :]
    inward = rdiff * (radius - 0.5 * spacing) / radius
    outward = rdiff * (radius + 0.5 * spacing) / radius
    sink = rdiff * spacing * spacing / (radius * radius)
    grow = 1.0 + sink
    KC[0] = inward
    KC[1] = outward
    KC[2] = grow / outward
    KC[3] = -1.0 / radius
    KC[4] = 1.0 / (radius * radius)
    KC[5] = inward / outward
    KC[6] = grow / inward
    KC[7] = outward / inward
    A0[...] = 66.0 - 30.0 * KC[4]

    lane1 = lax.broadcasted_iota(jnp.int32, (1, 128), 1)
    ones = jnp.ones((1, 128), F32)

    def march(i, carry):
        phi, p, psi, m = carry
        k = R - 1 - i
        PHI[pl.ds(i, 1), :] = phi
        PSI[pl.ds(k, 1), :] = psi
        DM[pl.ds(k, 1), :] = m
        p = KC[2, pl.ds(i, 1), :] * phi + KC[5, pl.ds(i, 1), :] * p
        m = KC[6, pl.ds(k, 1), :] * psi + KC[7, pl.ds(k, 1), :] * m
        DP[pl.ds(i, 1), :] = p
        return phi + p, p, psi + m, m

    lax.fori_loop(0, R, march, (ones, ones, ones, ones))
    weight = 1.0 / (KC[1] * (DP[...] * PSI[...] + PHI[...] * DM[...]))
    at_i = lax.broadcasted_iota(jnp.int32, (R, R), 0)
    at_j = lax.broadcasted_iota(jnp.int32, (R, R), 1)
    upper_part = jnp.transpose(PSI[...] * weight)[0:R, :]
    lower_part = jnp.transpose(PHI[...] * weight)[0:R, :]
    inverse = jnp.where(at_i <= at_j, PHI[:, 0:R] * upper_part, PSI[:, 0:R] * lower_part)
    SPK[0] = -KC[0, 0:1, :] * jnp.broadcast_to(inverse[:, 0:1], (R, 128))
    SPK[1] = -KC[1, R - 1 : R, :] * jnp.broadcast_to(inverse[:, R - 1 : R], (R, 128))
    inverse = inverse * (1.0 / SCALE)
    high = inverse.astype(bf)
    MA[:, 0:R] = high
    MA[:, R : 2 * R] = high
    MB[...] = (inverse - high.astype(F32)).astype(bf)
    TB[me, 0:1, :] = SPK[0, 0:1, :]
    TB[me, 1:2, :] = SPK[1, 0:1, :]
    TB[me, 2:3, :] = SPK[0, R - 1 : R, :]
    TB[me, 3:4, :] = SPK[1, R - 1 : R, :]
    TB[me, 4:8, :] = jnp.zeros((4, 128), F32)
    pl.semaphore_wait(barrier, n + 2)

    def tile_of(p):
        return near if p < 2 else far

    def az_first(p):
        e = p % 2
        return pltpu.make_async_remote_copy(
            src_ref=F.at[0, tile_of(p), pl.ds(edge_first[e] + 2, 2), pl.ds(PAD, R), :],
            dst_ref=F.at[0, tile_of(p), pl.ds((1 - side_of[e]) * (NTL + 2), 2), pl.ds(PAD, R), :],
            send_sem=a0_ss.at[p], recv_sem=a0_rs.at[p], device_id={"az": beside[e]},
            device_id_type=MESH)

    def az_copy(s, p):
        return pltpu.make_async_remote_copy(
            src_ref=YE.at[s - 1, p], dst_ref=HA.at[s - 1, p], send_sem=az_ss.at[s - 1, p],
            recv_sem=az_rs.at[s - 1, p], device_id={"az": beside[p % 2]},
            device_id_type=MESH)

    def lh_copy(s, p):
        return pltpu.make_async_remote_copy(
            src_ref=LS.at[s - 1, p], dst_ref=LR.at[s - 1, p], send_sem=lh_ss.at[s - 1, p],
            recv_sem=lh_rs.at[s - 1, p], device_id={"az": beside[p % 2]},
            device_id_type=MESH)

    def ax_copy(s, m):
        return pltpu.make_async_remote_copy(
            src_ref=PS.at[s, m], dst_ref=PR.at[s, m], send_sem=ax_ss.at[s, m],
            recv_sem=ax_rs.at[s, m], device_id={"ax": other}, device_id_type=MESH)

    def rad_send(buf, ss, rs, d):
        return pltpu.make_async_remote_copy(
            src_ref=buf.at[me], dst_ref=buf.at[me], send_sem=ss.at[d],
            recv_sem=rs.at[me], device_id={"rad": peers[d]}, device_id_type=MESH)

    def rad_recv(buf, ss, rs, d):
        return pltpu.make_async_remote_copy(
            src_ref=buf.at[me], dst_ref=buf.at[peers[d]], send_sem=ss.at[d],
            recv_sem=rs.at[peers[d]], device_id={"rad": peers[d]}, device_id_type=MESH)

    for j in edges:
        for t in range(2):
            v_copy(t, j).wait()
    for p in range(2):
        az_first(p).start()
    for c in row_copies:
        c.wait()
    for d in range(n - 1):
        rad_send(RB0, r0_ss, r0_rs, d).start()
        rad_send(TB, t_ss, t_rs, d).start()

    lane = lax.broadcasted_iota(jnp.int32, (CH, 128), 1)

    def members_of(m):
        if m is None:
            return [x for q in range(4) for x in members_of(q)]
        inner = [first_of[m] + i for i in range(GI)]
        layers = ([edge_first[m], edge_first[m] + 1] if m < 2 else []) + inner
        first = m * GI + 2 * min(m, 2)
        return [(first + i, j) for i, j in enumerate(layers)]

    def pack(s, m):
        b = lax.rem(s, 2)
        for c in range(R // CH):
            acc = jnp.zeros((CH, 128), F32)
            for i, j in members_of(m):
                edge = F[b, near, j + 2, pl.ds(PAD + c * CH, CH), :]
                acc = jnp.where(lane // 2 == i, pltpu.roll(edge, 2 * i + 2 * (1 - ax), 1), acc)
            PS[s, m or 0, pl.ds(c * CH, CH), :] = acc

    def unpack(s, m):
        for c in range(R // CH):
            rows = pl.ds(c * CH, CH)
            x = PR[s, jnp.where(s == 0, 0, m), rows, :]
            high = x.astype(bf).astype(F32)
            x = jnp.where(lane < 64, high, pltpu.roll(x - high, 64, 1))
            for i, j in members_of(m):
                FB[j, rows, pl.ds(512, 128)] = jnp.where((lane % 64) // 2 == i, x, 0.0).astype(bf)

    def split_store(j, rows, t, x):
        high = x.astype(bf)
        at = pl.multiple_of(t * 128, 128) if not isinstance(t, int) else t * 128
        FB[j, rows, pl.ds(at, 128)] = high
        FB[j, rows, pl.ds(256 + at, 128)] = (x - high.astype(F32)).astype(bf)

    for j in range(2, NTL - 2):
        for t in range(2):
            v_copy(t, j).wait()

    def first_split(j, carry):
        for t in range(2):
            for c in range(R // CH):
                rows = pl.ds(c * CH, CH)
                split_store(j, rows, t, F[0, t, j + 2, pl.ds(PAD + c * CH, CH), :])
        return carry

    pack(0, None)
    ax_copy(0, 0).start()
    lax.fori_loop(0, NTL, first_split, 0)
    for p in range(2, 4):
        az_first(p).start()

    def band(source, t):
        d = source - (128 * t + lax.broadcasted_iota(jnp.int32, (CH, 128), 1))
        slope = (jnp.where(d == 1, -32.0, 0.0) + jnp.where(d == -1, 32.0, 0.0)
                 + jnp.where(d == 2, 4.0, 0.0) + jnp.where(d == -2, -4.0, 0.0))
        curve = (jnp.where(jnp.abs(d) == 1, 16.0, 0.0) - jnp.where(jnp.abs(d) == 2, 1.0, 0.0))
        return slope.astype(bf), curve.astype(bf)

    here = lax.broadcasted_iota(jnp.int32, (CH, 128), 0)

    def bands(c, carry):
        r0 = pl.multiple_of(c * CH, CH)
        for t in range(2):
            slope, curve = band(here + c * CH, t)
            for q in range(2):
                BW[t, pl.ds(pl.multiple_of(q * 256 + r0, CH), CH), 0:128] = slope
                BW[t, pl.ds(pl.multiple_of(q * 256 + r0, CH), CH), 128:256] = curve
        return carry

    lax.fori_loop(0, 256 // CH, bands, 0)
    for t in range(2):
        slope, curve = band(jnp.where(ax == 0, 256 + here % 2, here % 2 - 2), t)
        for c in range(128 // CH):
            BW[t, pl.ds(512 + c * CH, CH), 0:128] = slope
            BW[t, pl.ds(512 + c * CH, CH), 128:256] = curve

    for q, (dst, scale) in enumerate(((RCF, -0.5 * SCALE), (ACF, None))):
        coef_copies[q].wait()
        for t in range(2):
            def convert(c, carry):
                rows = pl.ds(pl.multiple_of(c * 8, 8), 8)
                x = STB[q, rows, :, pl.ds(128 * t, 128)].astype(F32)
                dst[t, :, rows, :] = jnp.swapaxes(x if scale is None else x * scale, 0, 1)
                return carry

            lax.fori_loop(0, R // 8, convert, 0)

    for d in range(n - 1):
        rad_recv(RB0, r0_ss, r0_rs, d).wait_recv()
    below = jnp.maximum(me - 1, 0)
    above = jnp.minimum(me + 1, n - 1)
    low0 = jnp.where(me > 0, RB0[below, NTL : 2 * NTL, :], 0.0)
    high0 = jnp.where(me < n - 1, RB0[above, 0:NTL, :], 0.0)
    for j in range(NTL):
        for t in range(2):
            F[0, t, j + 2, PAD - 1 : PAD, :] = low0[j : j + 1, 128 * t : 128 * t + 128]
            F[0, t, j + 2, PAD + R : PAD + R + 1, :] = high0[j : j + 1, 128 * t : 128 * t + 128]

    for d in range(n - 1):
        rad_recv(TB, t_ss, t_rs, d).wait_recv()
    members = []
    for k in range(n):
        members.append((
            jnp.where(lane1 == 2 * k, 1.0, 0.0),
            jnp.where(lane1 == 2 * k + 1, 1.0, 0.0),
            tuple(TB[k, q : q + 1, :] for q in range(4)),
        ))
    lower_map, upper_map = interface_rows(members, me, n)
    for m in range(2 * n):
        for h, vec in enumerate((lower_map, upper_map)):
            val = jnp.sum(jnp.where(lane1 == m, vec, 0.0), axis=1, keepdims=True)
            CF[h, m // 2, m % 2 : m % 2 + 1, :] = jnp.broadcast_to(val, (1, 128))

    def right_side(b, t, j, r0, near_by, slope, curve):
        rows = pl.ds(PAD + r0, CH)
        at = pl.ds(r0, CH)
        f = F[b, t, j + 2, rows, :]
        lo = F[b, t, j + 2, pl.ds(PAD + r0 - 1, CH), :]
        up = F[b, t, j + 2, pl.ds(PAD + r0 + 1, CH), :]
        m2, m1, p1, p2 = near_by
        dt = 8.0 * (p1 - m1) - (p2 - m2)
        lt = 16.0 * (p1 + m1) - (p2 + m2)
        return (
            f * (A0[at, :] + KC[3, at, :] * dt) + KC[4, at, :] * lt
            + RCF[t, j, at, :] * (up - lo) + (ACF[t, j, at, :] * slope + curve)
        )

    def solve(q):
        return (jnp.dot(MA[...], q[...], preferred_element_type=F32)
                + jnp.dot(MB[...], q[0:R, :], preferred_element_type=F32))

    def put_q(q, r0, cols, x):
        high = x.astype(bf)
        q[pl.ds(r0, CH), cols] = high
        q[pl.ds(R + r0, CH), cols] = (x - high.astype(F32)).astype(bf)

    def stencil(dst, lhs):
        dst[near] = jnp.dot(lhs, BW[near], preferred_element_type=F32)
        dst[far] = jnp.dot(lhs[:, 0:512], BW[far, 0:512, :], preferred_element_type=F32)

    def ax_wait(s, m):
        if m == 0:
            ax_copy(s, m).wait()
        else:
            @pl.when(s > 0)
            def _():
                ax_copy(s, m).wait()

    def axial(s, k):
        unpack(s, k)
        stencil(SC, FB[pl.ds(first_of[k], GI)].reshape(GI * R, 640))

    def axial_edges(k):
        stencil(SCE.at[k], FB[pl.ds(edge_first[k], 2)].reshape(2 * R, 640))

    def edge_solve(s, p):
        side = p % 2
        b = lax.rem(s, 2)
        t = tile_of(p)

        halo = side_of[side] * (NTL + 2)

        @pl.when(s == 0)
        def _():
            az_first(p).wait_recv()

        @pl.when(s > 0)
        def _():
            for copy in (az_copy, lh_copy):
                copy(s, p).wait_recv()
            for i in range(2):
                cols = slice(i * 128, i * 128 + 128)
                low = LR[s - 1, p, 0:1, cols]
                high = LR[s - 1, p, 1:2, cols]
                for c in range(R // CH):
                    here = pl.ds(c * CH, CH)
                    rows = pl.ds(PAD + c * CH, CH)
                    F[b, t, halo + i, rows, :] = (
                        HA[s - 1, p, here, cols] - SPK[0, here, :] * low
                        - SPK[1, here, :] * high - F[1 - b, t, halo + i, rows, :])

        for i in range(2):
            j = edge_first[side] + i
            for c in range(R // CH):
                r0 = c * CH
                at = pl.ds(i * R + r0, CH)
                x = right_side(
                    b, t, j, r0,
                    [F[b, t, j + 2 + o, pl.ds(PAD + r0, CH), :] for o in (-2, -1, 1, 2)],
                    SCE[side, t, at, 0:128], SCE[side, t, at, 128:256])
                put_q(QE, r0, pl.ds(i * 128, 128), x)
        y = solve(QE)
        YE[s, p] = y
        RBE[s, p, me, 0:1, :] = y[0:1, :]
        RBE[s, p, me, 1:2, :] = y[R - 1 : R, :]
        for d in range(n - 1):
            rad_send(RBE.at[s, p], re_ss.at[s, p], re_rs.at[s, p], d).start()

        @pl.when(s < STEPS - 1)
        def _():
            az_copy(s + 1, p).start()

    def ends(buf, idx, width):
        res = []
        for h in range(2):
            total = None
            for k in range(n):
                coef = jnp.concatenate([CF[h, k]] * (width // 128), axis=1)
                term = coef * buf[(*idx, k)]
                total = term if total is None else total + term
            res.append(total[0:1, :] + total[1:2, :])
        return res

    def advance(b, t, j, y_of, low, high):
        for c in range(R // CH):
            here = pl.ds(c * CH, CH)
            rows = pl.ds(PAD + c * CH, CH)
            x = (y_of(here) - SPK[0, here, :] * low - SPK[1, here, :] * high - F[b, t, j + 2, rows, :])
            F[1 - b, t, j + 2, rows, :] = x
            split_store(j, here, t, x)
        F[1 - b, t, j + 2, PAD - 1 : PAD, :] = low - F[b, t, j + 2, PAD - 1 : PAD, :]
        F[1 - b, t, j + 2, PAD + R : PAD + R + 1, :] = high - F[b, t, j + 2, PAD + R : PAD + R + 1, :]

    def edge_finish(s, p):
        b = lax.rem(s, 2)
        t = tile_of(p)
        buf, ss, rs = RBE.at[s, p], re_ss.at[s, p], re_rs.at[s, p]
        for d in range(n - 1):
            rad_send(buf, ss, rs, d).wait_send()
        for d in range(n - 1):
            rad_recv(buf, ss, rs, d).wait_recv()
        low, high = ends(RBE, (s, p), 256)

        @pl.when(s == 0)
        def _():
            az_first(p).wait_send()

        @pl.when(s > 0)
        def _():
            az_copy(s, p).wait_send()
            lh_copy(s, p).wait_send()

        @pl.when(s < STEPS - 1)
        def _():
            LS[s, p, 0:1, :] = low
            LS[s, p, 1:2, :] = high
            lh_copy(s + 1, p).start()

        for i in range(2):
            cols = slice(i * 128, i * 128 + 128)
            advance(b, t, edge_first[p % 2] + i,
                    lambda here: YE[s, p, here, cols], low[:, cols], high[:, cols])

        for q in range(2):
            @pl.when(jnp.logical_and(s == STEPS - 1, parity == q))
            def _():
                for i in range(2):
                    o_copy(t, edge(p, q) + i).start()

    def inner_solve(s, k):
        b = lax.rem(s, 2)
        def rhs(i):
            j = first_of[k] + i
            for c in range(R // CH):
                for t in range(2):
                    r0 = c * CH
                    at = pl.ds(pl.multiple_of(i * R + r0, CH), CH)
                    x = right_side(
                        b, t, j, r0,
                        [F[b, t, j + 2 + o, pl.ds(PAD + r0, CH), :] for o in (-2, -1, 1, 2)],
                        SC[t, at, 0:128], SC[t, at, 128:256])
                    put_q(Q.at[i], r0, pl.ds(t * 128, 128), x)

        def close(i):
            y = solve(Q.at[i])
            Y[k, i] = y
            cols = pl.ds(pl.multiple_of(i * NZL, NZL), NZL)
            RBI[s, k, me, 0:1, cols] = y[0:1, :]
            RBI[s, k, me, 1:2, cols] = y[R - 1 : R, :]

        rhs(0)

        def body(i, c):
            close(i - 1)
            rhs(i)
            return c

        lax.fori_loop(1, GI, body, 0)
        close(GI - 1)
        for d in range(n - 1):
            rad_send(RBI.at[s, k], ri_ss.at[s, k], ri_rs.at[s, k], d).start()

    def inner_finish(s, k, then=None):
        b = lax.rem(s, 2)
        buf, ss, rs = RBI.at[s, k], ri_ss.at[s, k], ri_rs.at[s, k]
        for d in range(n - 1):
            rad_send(buf, ss, rs, d).wait_send()
        if then is not None:
            ax_wait(*then)
        for d in range(n - 1):
            rad_recv(buf, ss, rs, d).wait_recv()
        if then is not None:
            axial(*then)
        low, high = ends(RBI, (s, k), GI * NZL)
        for i in range(GI):
            for t in range(2):
                cols = slice(i * NZL + t * 128, i * NZL + t * 128 + 128)
                advance(b, t, first_of[k] + i,
                        lambda here: Y[k, i, here, pl.ds(t * 128, 128)],
                        low[:, cols], high[:, cols])

        for q in range(2):
            @pl.when(jnp.logical_and(s == STEPS - 1, parity == q))
            def _():
                for i in range(GI):
                    for t in range(2):
                        o_copy(t, group(k, q) + i).start()

    def send_axial(s, k):
        pack(s, k)
        ax_copy(s, k).start()

    def step(s, carry):
        for k in range(4):
            inner_solve(s, k)
            edge_solve(s, k)
            if k == 0:
                @pl.when(s > 0)
                def _():
                    inner_finish(s - 1, 3, (s, 1))
                    edge_finish(s - 1, 3)
                    send_axial(s, 3)

                @pl.when(s == 0)
                def _():
                    axial(s, 1)

                axial_edges(1)
            elif k < 3:
                inner_finish(s, k - 1, (s, k + 1))
                edge_finish(s, k - 1)

                @pl.when(s < STEPS - 1)
                def _():
                    send_axial(s + 1, k - 1)
            else:
                @pl.when(s < STEPS - 1)
                def _():
                    inner_finish(s, 2, (s + 1, 0))

                @pl.when(s == STEPS - 1)
                def _():
                    inner_finish(s, 2)

                edge_finish(s, 2)

                @pl.when(s < STEPS - 1)
                def _():
                    send_axial(s + 1, 2)
                    axial_edges(0)
        return carry

    ax_wait(0, 0)
    axial(0, 0)
    axial_edges(0)
    lax.fori_loop(0, STEPS, step, 0)
    inner_finish(STEPS - 1, 3)
    edge_finish(STEPS - 1, 3)
    for j in range(NTL):
        for t in range(2):
            o_copy(t, j).wait()
    for d in range(n - 1):
        rad_send(RB0, r0_ss, r0_rs, d).wait_send()
        rad_send(TB, t_ss, t_rs, d).wait_send()


def local(n, naz, velocity, radial_courant, axial_courant, radial_diffusion):
    R, NTL, NZL = velocity.shape
    S = STEPS
    GI = (NTL - 4) // 4
    dma = pltpu.SemaphoreType.DMA
    bf = jnp.bfloat16
    hbm = pl.BlockSpec(memory_space=pl.ANY)
    return pl.pallas_call(
        functools.partial(kernel, n, naz, R, NTL, NZL),
        out_shape=jax.ShapeDtypeStruct((R, NTL, NZL), F32),
        in_specs=[hbm, hbm, hbm, pl.BlockSpec(memory_space=pltpu.VMEM)],
        out_specs=hbm,
        scratch_shapes=[
            pltpu.VMEM((2, 2, NTL + 4, R + 2 * PAD, 128), F32),
            pltpu.VMEM((NTL, R, 640), bf),
            pltpu.VMEM((S - 1, 4, R, 256), F32),
            pltpu.VMEM((S - 1, 4, 2, 256), F32),
            pltpu.VMEM((S - 1, 4, 2, 256), F32),
            pltpu.VMEM((4, GI, R, NZL), F32),
            pltpu.VMEM((S, 4, R, 256), F32),
            pltpu.VMEM((GI, 2 * R, NZL), bf),
            pltpu.VMEM((2 * R, 256), bf),
            pltpu.VMEM((2, GI * R, 256), F32),
            pltpu.VMEM((2, 2, 2 * R, 256), F32),
            pltpu.VMEM((2, NTL, R, 128), F32),
            pltpu.VMEM((2, NTL, R, 128), F32),
            pltpu.VMEM((2, 640, 256), bf),
            pltpu.VMEM((S, 4, R, 128), F32),
            pltpu.VMEM((S, 4, R, 128), F32),
            pltpu.VMEM((n, 2 * NTL, NZL), F32),
            pltpu.VMEM((S, 4, n, 2, 256), F32),
            pltpu.VMEM((S, 4, n, 2, GI * NZL), F32),
            pltpu.VMEM((n, 8, 128), F32),
            pltpu.VMEM((R, 2 * R), bf),
            pltpu.VMEM((R, R), bf),
            pltpu.VMEM((8, R, 128), F32),
            pltpu.VMEM((R, 128), F32),
            pltpu.VMEM((R, 128), F32),
            pltpu.VMEM((R, 128), F32),
            pltpu.VMEM((R, 128), F32),
            pltpu.VMEM((R, 128), F32),
            pltpu.VMEM((2, R, 128), F32),
            pltpu.VMEM((2, n, 2, 128), F32),
            pltpu.VMEM((2, R, NTL, NZL), bf),
            dma((4,)), dma((4,)), dma((S - 1, 4)), dma((S - 1, 4)), dma((S - 1, 4)), dma((S - 1, 4)),
            dma((S, 4)), dma((S, 4)),
            dma((n,)), dma((n,)), dma((S, 4, n)), dma((S, 4, n)),
            dma((S, 4, n)), dma((S, 4, n)), dma((n,)), dma((n,)),
            dma((2, NTL)), dma((2,)), dma((2,)), dma((2, NTL)),
        ],
        compiler_params=pltpu.CompilerParams(
            collective_id=0, has_side_effects=True, vmem_limit_bytes=58 * 1024 * 1024),
    )(velocity, radial_courant, axial_courant, radial_diffusion.reshape(1, R))


def solution(mesh):
    return jax.shard_map(
        functools.partial(local, mesh.shape["rad"], mesh.shape["az"]),
        mesh=mesh,
        in_specs=(P("rad", "az", "ax"), P("rad", "az", "ax"), P("rad", "az", "ax"), P("rad")),
        out_specs=P("rad", "az", "ax"),
        check_vma=False,
    )
```

```python
import functools

import jax
import jax.numpy as jnp
from jax import lax
from jax.experimental import pallas as pl
from jax.experimental.pallas import tpu as pltpu
from jax.sharding import PartitionSpec as P

NR = 512
STEPS = 6
F32 = jnp.float32
MESH = pl.DeviceIdType.MESH
PAD = 8
CH = 16


def join_slabs(left, right):
    head_l, tail_l, tl = left
    head_r, tail_r, tr = right
    divisor = 1.0 - tl[3] * tr[0]
    mid_value = (tail_l - tl[3] * head_r) / divisor
    mid_left = tl[2] / divisor
    mid_right = -tl[3] * tr[1] / divisor
    next_value = head_r - tr[0] * mid_value
    next_left = -tr[0] * mid_left
    next_right = tr[1] - tr[0] * mid_right
    return (
        head_l - tl[1] * next_value,
        tail_r - tr[2] * mid_value,
        (
            tl[0] - tl[1] * next_left,
            -tl[1] * next_right,
            -tr[2] * mid_left,
            tr[3] - tr[2] * mid_right,
        ),
    )


def interface_rows(members, me, n):
    zero = jnp.zeros_like(members[0][0])
    identity = (zero, zero, (zero, zero - 1.0, zero - 1.0, zero))

    def choose(cond, a, b):
        return jax.tree.map(lambda x, y: jnp.where(cond, x, y), a, b)

    prefix = identity
    own = members[0]
    for k in range(n):
        own = choose(k == me, members[k], own)
        prefix = choose(k < me, join_slabs(prefix, members[k]), prefix)
    suffix = identity
    for k in range(n - 1, -1, -1):
        suffix = choose(k > me, join_slabs(members[k], suffix), suffix)
    combined = join_slabs(own, suffix)
    lower = (prefix[1] - prefix[2][3] * combined[0]) / (1.0 - prefix[2][3] * combined[2][0])
    upper = (suffix[0] - suffix[2][0] * (own[1] - own[2][2] * lower)) / (
        1.0 - suffix[2][0] * own[2][3]
    )
    return lower, upper


SCALE = 48.0


def kernel(
    n, naz, R, NTL, NZL,
    v, rc, ac, rd, out,
    F, FB, HA, LS, LR, Y, YE, Q, QE, SC, SCE, RCF, ACF, BW, PS, PR, RB0, RBE, RBI, TB, MA, MB, KC,
    PHI, PSI, DP, DM, A0, SPK, CF, STB,
    a0_ss, a0_rs, az_ss, az_rs, lh_ss, lh_rs, ax_ss, ax_rs, r0_ss, r0_rs, re_ss, re_rs, ri_ss, ri_rs, t_ss, t_rs,
    v_s, rb_s, cb_s, o_s,
):
    me = lax.axis_index("rad")
    az = lax.axis_index("az")
    ax = lax.axis_index("ax")
    left = lax.rem(az + naz - 1, naz)
    right = lax.rem(az + 1, naz)
    other = 1 - ax
    near, far = 1 - ax, ax
    peers = [lax.rem(me + d, n) for d in range(1, n)]
    GI = (NTL - 4) // 4
    parity = lax.rem(az, 2)

    def group(k, q):
        lowest = (2, 2 + 3 * GI, 2 + GI, 2 + 2 * GI)
        return lowest[k] if q == 0 else lowest[k ^ 1]

    def edge(p, q):
        return (NTL - 2) * ((p % 2) ^ q)

    first_of = [group(k, 0) + parity * (group(k, 1) - group(k, 0)) for k in range(4)]
    edge_first = [edge(p, 0) + parity * (edge(p, 1) - edge(p, 0)) for p in range(2)]
    side_of = [p + parity * (1 - 2 * p) for p in range(2)]
    beside = [lax.rem(az + naz - 1 + 2 * side_of[p], naz) for p in range(2)]
    bf = jnp.bfloat16

    def v_copy(t, j):
        return pltpu.make_async_copy(
            v.at[:, j, pl.ds(128 * t, 128)], F.at[0, t, j + 2, pl.ds(PAD, R), :], v_s.at[t, j])

    def o_copy(t, j):
        return pltpu.make_async_copy(
            F.at[STEPS % 2, t, j + 2, pl.ds(PAD, R), :],
            out.at[:, j, pl.ds(pl.multiple_of(128 * t, 128), 128)], o_s.at[t, j])

    barrier = pltpu.get_barrier_semaphore()
    for p in peers:
        pl.semaphore_signal(barrier, inc=1, device_id={"rad": p}, device_id_type=MESH)
    for p in (left, right):
        pl.semaphore_signal(barrier, inc=1, device_id={"az": p}, device_id_type=MESH)
    pl.semaphore_signal(barrier, inc=1, device_id={"ax": other}, device_id_type=MESH)

    edges = (0, 1, NTL - 2, NTL - 1)
    for j in edges:
        for t in range(2):
            v_copy(t, j).start()
    row_copies = [
        pltpu.make_async_copy(v.at[r], RB0.at[me, pl.ds(q * NTL, NTL), :], rb_s.at[q])
        for q, r in enumerate((0, R - 1))]
    for c in row_copies:
        c.start()
    for j in range(2, NTL - 2):
        for t in range(2):
            v_copy(t, j).start()
    coef_copies = [
        pltpu.make_async_copy(src, STB.at[q], cb_s.at[q]) for q, src in enumerate((rc, ac))]
    for c in coef_copies:
        c.start()

    row = lax.broadcasted_iota(jnp.int32, (R, 128), 0)
    spacing = 1.0 / (NR + 1)
    radius = 1.0 + ((me * R + row).astype(F32) + 1.0) * spacing
    rdiff = jnp.transpose(jnp.broadcast_to(
        jnp.concatenate([rd[...]] * (128 // R), axis=1), (128, 128)))[0:R, :]
    inward = rdiff * (radius - 0.5 * spacing) / radius
    outward = rdiff * (radius + 0.5 * spacing) / radius
    sink = rdiff * spacing * spacing / (radius * radius)
    grow = 1.0 + sink
    KC[0] = inward
    KC[1] = outward
    KC[2] = grow / outward
    KC[3] = -1.0 / radius
    KC[4] = 1.0 / (radius * radius)
    KC[5] = inward / outward
    KC[6] = grow / inward
    KC[7] = outward / inward
    A0[...] = 66.0 - 30.0 * KC[4]

    lane1 = lax.broadcasted_iota(jnp.int32, (1, 128), 1)
    ones = jnp.ones((1, 128), F32)

    def march(i, carry):
        phi, p, psi, m = carry
        k = R - 1 - i
        PHI[pl.ds(i, 1), :] = phi
        PSI[pl.ds(k, 1), :] = psi
        DM[pl.ds(k, 1), :] = m
        p = KC[2, pl.ds(i, 1), :] * phi + KC[5, pl.ds(i, 1), :] * p
        m = KC[6, pl.ds(k, 1), :] * psi + KC[7, pl.ds(k, 1), :] * m
        DP[pl.ds(i, 1), :] = p
        return phi + p, p, psi + m, m

    lax.fori_loop(0, R, march, (ones, ones, ones, ones))
    weight = 1.0 / (KC[1] * (DP[...] * PSI[...] + PHI[...] * DM[...]))
    at_i = lax.broadcasted_iota(jnp.int32, (R, R), 0)
    at_j = lax.broadcasted_iota(jnp.int32, (R, R), 1)
    upper_part = jnp.transpose(PSI[...] * weight)[0:R, :]
    lower_part = jnp.transpose(PHI[...] * weight)[0:R, :]
    inverse = jnp.where(at_i <= at_j, PHI[:, 0:R] * upper_part, PSI[:, 0:R] * lower_part)
    SPK[0] = -KC[0, 0:1, :] * jnp.broadcast_to(inverse[:, 0:1], (R, 128))
    SPK[1] = -KC[1, R - 1 : R, :] * jnp.broadcast_to(inverse[:, R - 1 : R], (R, 128))
    inverse = inverse * (1.0 / SCALE)
    high = inverse.astype(bf)
    MA[:, 0:R] = high
    MA[:, R : 2 * R] = high
    MB[...] = (inverse - high.astype(F32)).astype(bf)
    TB[me, 0:1, :] = SPK[0, 0:1, :]
    TB[me, 1:2, :] = SPK[1, 0:1, :]
    TB[me, 2:3, :] = SPK[0, R - 1 : R, :]
    TB[me, 3:4, :] = SPK[1, R - 1 : R, :]
    TB[me, 4:8, :] = jnp.zeros((4, 128), F32)
    pl.semaphore_wait(barrier, n + 2)

    def tile_of(p):
        return near if p < 2 else far

    def az_first(p):
        e = p % 2
        return pltpu.make_async_remote_copy(
            src_ref=F.at[0, tile_of(p), pl.ds(edge_first[e] + 2, 2), pl.ds(PAD, R), :],
            dst_ref=F.at[0, tile_of(p), pl.ds((1 - side_of[e]) * (NTL + 2), 2), pl.ds(PAD, R), :],
            send_sem=a0_ss.at[p], recv_sem=a0_rs.at[p], device_id={"az": beside[e]},
            device_id_type=MESH)

    def az_copy(s, p):
        return pltpu.make_async_remote_copy(
            src_ref=YE.at[s - 1, p], dst_ref=HA.at[s - 1, p], send_sem=az_ss.at[s - 1, p],
            recv_sem=az_rs.at[s - 1, p], device_id={"az": beside[p % 2]},
            device_id_type=MESH)

    def lh_copy(s, p):
        return pltpu.make_async_remote_copy(
            src_ref=LS.at[s - 1, p], dst_ref=LR.at[s - 1, p], send_sem=lh_ss.at[s - 1, p],
            recv_sem=lh_rs.at[s - 1, p], device_id={"az": beside[p % 2]},
            device_id_type=MESH)

    def ax_copy(s, m):
        return pltpu.make_async_remote_copy(
            src_ref=PS.at[s, m], dst_ref=PR.at[s, m], send_sem=ax_ss.at[s, m],
            recv_sem=ax_rs.at[s, m], device_id={"ax": other}, device_id_type=MESH)

    def rad_send(buf, ss, rs, d):
        return pltpu.make_async_remote_copy(
            src_ref=buf.at[me], dst_ref=buf.at[me], send_sem=ss.at[d],
            recv_sem=rs.at[me], device_id={"rad": peers[d]}, device_id_type=MESH)

    def rad_recv(buf, ss, rs, d):
        return pltpu.make_async_remote_copy(
            src_ref=buf.at[me], dst_ref=buf.at[peers[d]], send_sem=ss.at[d],
            recv_sem=rs.at[peers[d]], device_id={"rad": peers[d]}, device_id_type=MESH)

    for j in edges:
        for t in range(2):
            v_copy(t, j).wait()
    for p in range(4):
        az_first(p).start()
    for c in row_copies:
        c.wait()
    for d in range(n - 1):
        rad_send(RB0, r0_ss, r0_rs, d).start()
        rad_send(TB, t_ss, t_rs, d).start()

    lane = lax.broadcasted_iota(jnp.int32, (CH, 128), 1)

    def members_of(m):
        if m is None:
            return [x for q in range(4) for x in members_of(q)]
        inner = [first_of[m] + i for i in range(GI)]
        layers = ([edge_first[m], edge_first[m] + 1] if m < 2 else []) + inner
        first = m * GI + 2 * min(m, 2)
        return [(first + i, j) for i, j in enumerate(layers)]

    def pack(s, m):
        b = lax.rem(s, 2)
        for c in range(R // CH):
            acc = jnp.zeros((CH, 128), F32)
            for i, j in members_of(m):
                edge = F[b, near, j + 2, pl.ds(PAD + c * CH, CH), :]
                acc = jnp.where(lane // 2 == i, pltpu.roll(edge, 2 * i + 2 * (1 - ax), 1), acc)
            PS[s, m or 0, pl.ds(c * CH, CH), :] = acc

    def unpack(s, m):
        for c in range(R // CH):
            rows = pl.ds(c * CH, CH)
            x = PR[s, jnp.where(s == 0, 0, m), rows, :]
            high = x.astype(bf).astype(F32)
            x = jnp.where(lane < 64, high, pltpu.roll(x - high, 64, 1))
            for i, j in members_of(m):
                FB[j, rows, pl.ds(512, 128)] = jnp.where((lane % 64) // 2 == i, x, 0.0).astype(bf)

    def split_store(j, rows, t, x):
        high = x.astype(bf)
        at = pl.multiple_of(t * 128, 128) if not isinstance(t, int) else t * 128
        FB[j, rows, pl.ds(at, 128)] = high
        FB[j, rows, pl.ds(256 + at, 128)] = (x - high.astype(F32)).astype(bf)

    for j in range(2, NTL - 2):
        for t in range(2):
            v_copy(t, j).wait()

    def first_split(j, carry):
        for t in range(2):
            for c in range(R // CH):
                rows = pl.ds(c * CH, CH)
                split_store(j, rows, t, F[0, t, j + 2, pl.ds(PAD + c * CH, CH), :])
        return carry

    pack(0, None)
    ax_copy(0, 0).start()
    lax.fori_loop(0, NTL, first_split, 0)

    def band(source, t):
        d = source - (128 * t + lax.broadcasted_iota(jnp.int32, (CH, 128), 1))
        slope = (jnp.where(d == 1, -32.0, 0.0) + jnp.where(d == -1, 32.0, 0.0)
                 + jnp.where(d == 2, 4.0, 0.0) + jnp.where(d == -2, -4.0, 0.0))
        curve = (jnp.where(jnp.abs(d) == 1, 16.0, 0.0) - jnp.where(jnp.abs(d) == 2, 1.0, 0.0))
        return slope.astype(bf), curve.astype(bf)

    here = lax.broadcasted_iota(jnp.int32, (CH, 128), 0)

    def bands(c, carry):
        r0 = pl.multiple_of(c * CH, CH)
        for t in range(2):
            slope, curve = band(here + c * CH, t)
            for q in range(2):
                BW[t, pl.ds(pl.multiple_of(q * 256 + r0, CH), CH), 0:128] = slope
                BW[t, pl.ds(pl.multiple_of(q * 256 + r0, CH), CH), 128:256] = curve
        return carry

    lax.fori_loop(0, 256 // CH, bands, 0)
    for t in range(2):
        slope, curve = band(jnp.where(ax == 0, 256 + here % 2, here % 2 - 2), t)
        for c in range(128 // CH):
            BW[t, pl.ds(512 + c * CH, CH), 0:128] = slope
            BW[t, pl.ds(512 + c * CH, CH), 128:256] = curve

    for q, (dst, scale) in enumerate(((RCF, -0.5 * SCALE), (ACF, None))):
        coef_copies[q].wait()
        for t in range(2):
            def convert(c, carry):
                rows = pl.ds(pl.multiple_of(c * 8, 8), 8)
                x = STB[q, rows, :, pl.ds(128 * t, 128)].astype(F32)
                dst[t, :, rows, :] = jnp.swapaxes(x if scale is None else x * scale, 0, 1)
                return carry

            lax.fori_loop(0, R // 8, convert, 0)

    for d in range(n - 1):
        rad_recv(RB0, r0_ss, r0_rs, d).wait_recv()
    below = jnp.maximum(me - 1, 0)
    above = jnp.minimum(me + 1, n - 1)
    low0 = jnp.where(me > 0, RB0[below, NTL : 2 * NTL, :], 0.0)
    high0 = jnp.where(me < n - 1, RB0[above, 0:NTL, :], 0.0)
    for j in range(NTL):
        for t in range(2):
            F[0, t, j + 2, PAD - 1 : PAD, :] = low0[j : j + 1, 128 * t : 128 * t + 128]
            F[0, t, j + 2, PAD + R : PAD + R + 1, :] = high0[j : j + 1, 128 * t : 128 * t + 128]

    for d in range(n - 1):
        rad_recv(TB, t_ss, t_rs, d).wait_recv()
    members = []
    for k in range(n):
        members.append((
            jnp.where(lane1 == 2 * k, 1.0, 0.0),
            jnp.where(lane1 == 2 * k + 1, 1.0, 0.0),
            tuple(TB[k, q : q + 1, :] for q in range(4)),
        ))
    lower_map, upper_map = interface_rows(members, me, n)
    for m in range(2 * n):
        for h, vec in enumerate((lower_map, upper_map)):
            val = jnp.sum(jnp.where(lane1 == m, vec, 0.0), axis=1, keepdims=True)
            CF[h, m // 2, m % 2 : m % 2 + 1, :] = jnp.broadcast_to(val, (1, 128))

    def right_side(b, t, j, r0, near_by, slope, curve):
        rows = pl.ds(PAD + r0, CH)
        at = pl.ds(r0, CH)
        f = F[b, t, j + 2, rows, :]
        lo = F[b, t, j + 2, pl.ds(PAD + r0 - 1, CH), :]
        up = F[b, t, j + 2, pl.ds(PAD + r0 + 1, CH), :]
        m2, m1, p1, p2 = near_by
        dt = 8.0 * (p1 - m1) - (p2 - m2)
        lt = 16.0 * (p1 + m1) - (p2 + m2)
        return (
            f * (A0[at, :] + KC[3, at, :] * dt) + KC[4, at, :] * lt
            + RCF[t, j, at, :] * (up - lo) + (ACF[t, j, at, :] * slope + curve)
        )

    def solve(q):
        return (jnp.dot(MA[...], q[...], preferred_element_type=F32)
                + jnp.dot(MB[...], q[0:R, :], preferred_element_type=F32))

    def put_q(q, r0, cols, x):
        high = x.astype(bf)
        q[pl.ds(r0, CH), cols] = high
        q[pl.ds(R + r0, CH), cols] = (x - high.astype(F32)).astype(bf)

    def stencil(dst, lhs):
        dst[near] = jnp.dot(lhs, BW[near], preferred_element_type=F32)
        dst[far] = jnp.dot(lhs[:, 0:512], BW[far, 0:512, :], preferred_element_type=F32)

    def ax_wait(s, m):
        if m == 0:
            ax_copy(s, m).wait()
        else:
            @pl.when(s > 0)
            def _():
                ax_copy(s, m).wait()

    def axial(s, k):
        unpack(s, k)
        stencil(SC, FB[pl.ds(first_of[k], GI)].reshape(GI * R, 640))

    def axial_edges(k):
        stencil(SCE.at[k], FB[pl.ds(edge_first[k], 2)].reshape(2 * R, 640))

    def edge_solve(s, p):
        side = p % 2
        b = lax.rem(s, 2)
        t = tile_of(p)

        halo = side_of[side] * (NTL + 2)

        @pl.when(s == 0)
        def _():
            az_first(p).wait_recv()

        @pl.when(s > 0)
        def _():
            for copy in (az_copy, lh_copy):
                copy(s, p).wait_recv()
            for i in range(2):
                cols = slice(i * 128, i * 128 + 128)
                low = LR[s - 1, p, 0:1, cols]
                high = LR[s - 1, p, 1:2, cols]
                for c in range(R // CH):
                    here = pl.ds(c * CH, CH)
                    rows = pl.ds(PAD + c * CH, CH)
                    F[b, t, halo + i, rows, :] = (
                        HA[s - 1, p, here, cols] - SPK[0, here, :] * low
                        - SPK[1, here, :] * high - F[1 - b, t, halo + i, rows, :])

        for i in range(2):
            j = edge_first[side] + i
            for c in range(R // CH):
                r0 = c * CH
                at = pl.ds(i * R + r0, CH)
                x = right_side(
                    b, t, j, r0,
                    [F[b, t, j + 2 + o, pl.ds(PAD + r0, CH), :] for o in (-2, -1, 1, 2)],
                    SCE[side, t, at, 0:128], SCE[side, t, at, 128:256])
                put_q(QE, r0, pl.ds(i * 128, 128), x)
        y = solve(QE)
        YE[s, p] = y
        RBE[s, p, me, 0:1, :] = y[0:1, :]
        RBE[s, p, me, 1:2, :] = y[R - 1 : R, :]
        for d in range(n - 1):
            rad_send(RBE.at[s, p], re_ss.at[s, p], re_rs.at[s, p], d).start()

        @pl.when(s < STEPS - 1)
        def _():
            az_copy(s + 1, p).start()

    def ends(buf, idx, width):
        res = []
        for h in range(2):
            total = None
            for k in range(n):
                coef = jnp.concatenate([CF[h, k]] * (width // 128), axis=1)
                term = coef * buf[(*idx, k)]
                total = term if total is None else total + term
            res.append(total[0:1, :] + total[1:2, :])
        return res

    def advance(b, t, j, y_of, low, high):
        for c in range(R // CH):
            here = pl.ds(c * CH, CH)
            rows = pl.ds(PAD + c * CH, CH)
            x = (y_of(here) - SPK[0, here, :] * low - SPK[1, here, :] * high - F[b, t, j + 2, rows, :])
            F[1 - b, t, j + 2, rows, :] = x
            split_store(j, here, t, x)
        F[1 - b, t, j + 2, PAD - 1 : PAD, :] = low - F[b, t, j + 2, PAD - 1 : PAD, :]
        F[1 - b, t, j + 2, PAD + R : PAD + R + 1, :] = high - F[b, t, j + 2, PAD + R : PAD + R + 1, :]

    def edge_finish(s, p):
        b = lax.rem(s, 2)
        t = tile_of(p)
        buf, ss, rs = RBE.at[s, p], re_ss.at[s, p], re_rs.at[s, p]
        for d in range(n - 1):
            rad_send(buf, ss, rs, d).wait_send()
        for d in range(n - 1):
            rad_recv(buf, ss, rs, d).wait_recv()
        low, high = ends(RBE, (s, p), 256)

        @pl.when(s == 0)
        def _():
            az_first(p).wait_send()

        @pl.when(s > 0)
        def _():
            az_copy(s, p).wait_send()
            lh_copy(s, p).wait_send()

        @pl.when(s < STEPS - 1)
        def _():
            LS[s, p, 0:1, :] = low
            LS[s, p, 1:2, :] = high
            lh_copy(s + 1, p).start()

        for i in range(2):
            cols = slice(i * 128, i * 128 + 128)
            advance(b, t, edge_first[p % 2] + i,
                    lambda here: YE[s, p, here, cols], low[:, cols], high[:, cols])

        for q in range(2):
            @pl.when(jnp.logical_and(s == STEPS - 1, parity == q))
            def _():
                for i in range(2):
                    o_copy(t, edge(p, q) + i).start()

    def inner_solve(s, k):
        b = lax.rem(s, 2)
        def rhs(i):
            j = first_of[k] + i
            for c in range(R // CH):
                for t in range(2):
                    r0 = c * CH
                    at = pl.ds(pl.multiple_of(i * R + r0, CH), CH)
                    x = right_side(
                        b, t, j, r0,
                        [F[b, t, j + 2 + o, pl.ds(PAD + r0, CH), :] for o in (-2, -1, 1, 2)],
                        SC[t, at, 0:128], SC[t, at, 128:256])
                    put_q(Q.at[i], r0, pl.ds(t * 128, 128), x)

        def close(i):
            y = solve(Q.at[i])
            Y[k, i] = y
            cols = pl.ds(pl.multiple_of(i * NZL, NZL), NZL)
            RBI[s, k, me, 0:1, cols] = y[0:1, :]
            RBI[s, k, me, 1:2, cols] = y[R - 1 : R, :]

        rhs(0)

        def body(i, c):
            close(i - 1)
            rhs(i)
            return c

        lax.fori_loop(1, GI, body, 0)
        close(GI - 1)
        for d in range(n - 1):
            rad_send(RBI.at[s, k], ri_ss.at[s, k], ri_rs.at[s, k], d).start()

    def inner_finish(s, k, then=None):
        b = lax.rem(s, 2)
        buf, ss, rs = RBI.at[s, k], ri_ss.at[s, k], ri_rs.at[s, k]
        for d in range(n - 1):
            rad_send(buf, ss, rs, d).wait_send()
        if then is not None:
            ax_wait(*then)
        for d in range(n - 1):
            rad_recv(buf, ss, rs, d).wait_recv()
        if then is not None:
            axial(*then)
        low, high = ends(RBI, (s, k), GI * NZL)
        for i in range(GI):
            for t in range(2):
                cols = slice(i * NZL + t * 128, i * NZL + t * 128 + 128)
                advance(b, t, first_of[k] + i,
                        lambda here: Y[k, i, here, pl.ds(t * 128, 128)],
                        low[:, cols], high[:, cols])

        for q in range(2):
            @pl.when(jnp.logical_and(s == STEPS - 1, parity == q))
            def _():
                for i in range(GI):
                    for t in range(2):
                        o_copy(t, group(k, q) + i).start()

    def send_axial(s, k):
        pack(s, k)
        ax_copy(s, k).start()

    def step(s, carry):
        for k in range(4):
            inner_solve(s, k)
            edge_solve(s, k)
            if k == 0:
                @pl.when(s > 0)
                def _():
                    edge_finish(s - 1, 3)
                    inner_finish(s - 1, 3, (s, 1))
                    send_axial(s, 3)

                @pl.when(s == 0)
                def _():
                    axial(s, 1)

                axial_edges(1)
            elif k < 3:
                edge_finish(s, k - 1)
                inner_finish(s, k - 1, (s, k + 1))

                @pl.when(s < STEPS - 1)
                def _():
                    send_axial(s + 1, k - 1)
            else:
                @pl.when(s < STEPS - 1)
                def _():
                    inner_finish(s, 2, (s + 1, 0))

                @pl.when(s == STEPS - 1)
                def _():
                    inner_finish(s, 2)

                edge_finish(s, 2)

                @pl.when(s < STEPS - 1)
                def _():
                    send_axial(s + 1, 2)
                    axial_edges(0)
        return carry

    ax_wait(0, 0)
    axial(0, 0)
    axial_edges(0)
    lax.fori_loop(0, STEPS, step, 0)
    inner_finish(STEPS - 1, 3)
    edge_finish(STEPS - 1, 3)
    for j in range(NTL):
        for t in range(2):
            o_copy(t, j).wait()
    for d in range(n - 1):
        rad_send(RB0, r0_ss, r0_rs, d).wait_send()
        rad_send(TB, t_ss, t_rs, d).wait_send()


def local(n, naz, velocity, radial_courant, axial_courant, radial_diffusion):
    R, NTL, NZL = velocity.shape
    S = STEPS
    GI = (NTL - 4) // 4
    dma = pltpu.SemaphoreType.DMA
    bf = jnp.bfloat16
    hbm = pl.BlockSpec(memory_space=pl.ANY)
    return pl.pallas_call(
        functools.partial(kernel, n, naz, R, NTL, NZL),
        out_shape=jax.ShapeDtypeStruct((R, NTL, NZL), F32),
        in_specs=[hbm, hbm, hbm, pl.BlockSpec(memory_space=pltpu.VMEM)],
        out_specs=hbm,
        scratch_shapes=[
            pltpu.VMEM((2, 2, NTL + 4, R + 2 * PAD, 128), F32),
            pltpu.VMEM((NTL, R, 640), bf),
            pltpu.VMEM((S - 1, 4, R, 256), F32),
            pltpu.VMEM((S - 1, 4, 2, 256), F32),
            pltpu.VMEM((S - 1, 4, 2, 256), F32),
            pltpu.VMEM((4, GI, R, NZL), F32),
            pltpu.VMEM((S, 4, R, 256), F32),
            pltpu.VMEM((GI, 2 * R, NZL), bf),
            pltpu.VMEM((2 * R, 256), bf),
            pltpu.VMEM((2, GI * R, 256), F32),
            pltpu.VMEM((2, 2, 2 * R, 256), F32),
            pltpu.VMEM((2, NTL, R, 128), F32),
            pltpu.VMEM((2, NTL, R, 128), F32),
            pltpu.VMEM((2, 640, 256), bf),
            pltpu.VMEM((S, 4, R, 128), F32),
            pltpu.VMEM((S, 4, R, 128), F32),
            pltpu.VMEM((n, 2 * NTL, NZL), F32),
            pltpu.VMEM((S, 4, n, 2, 256), F32),
            pltpu.VMEM((S, 4, n, 2, GI * NZL), F32),
            pltpu.VMEM((n, 8, 128), F32),
            pltpu.VMEM((R, 2 * R), bf),
            pltpu.VMEM((R, R), bf),
            pltpu.VMEM((8, R, 128), F32),
            pltpu.VMEM((R, 128), F32),
            pltpu.VMEM((R, 128), F32),
            pltpu.VMEM((R, 128), F32),
            pltpu.VMEM((R, 128), F32),
            pltpu.VMEM((R, 128), F32),
            pltpu.VMEM((2, R, 128), F32),
            pltpu.VMEM((2, n, 2, 128), F32),
            pltpu.VMEM((2, R, NTL, NZL), bf),
            dma((4,)), dma((4,)), dma((S - 1, 4)), dma((S - 1, 4)), dma((S - 1, 4)), dma((S - 1, 4)),
            dma((S, 4)), dma((S, 4)),
            dma((n,)), dma((n,)), dma((S, 4, n)), dma((S, 4, n)),
            dma((S, 4, n)), dma((S, 4, n)), dma((n,)), dma((n,)),
            dma((2, NTL)), dma((2,)), dma((2,)), dma((2, NTL)),
        ],
        compiler_params=pltpu.CompilerParams(
            collective_id=0, has_side_effects=True, vmem_limit_bytes=58 * 1024 * 1024),
    )(velocity, radial_courant, axial_courant, radial_diffusion.reshape(1, R))


def solution(mesh):
    return jax.shard_map(
        functools.partial(local, mesh.shape["rad"], mesh.shape["az"]),
        mesh=mesh,
        in_specs=(P("rad", "az", "ax"), P("rad", "az", "ax"), P("rad", "az", "ax"), P("rad")),
        out_specs=P("rad", "az", "ax"),
        check_vma=False,
    )
```

```python
import functools

import jax
import jax.numpy as jnp
from jax import lax
from jax.experimental import pallas as pl
from jax.experimental.pallas import tpu as pltpu
from jax.sharding import PartitionSpec as P

NR = 512
STEPS = 6
F32 = jnp.float32
MESH = pl.DeviceIdType.MESH
PAD = 8
CH = 16


def join_slabs(left, right):
    head_l, tail_l, tl = left
    head_r, tail_r, tr = right
    divisor = 1.0 - tl[3] * tr[0]
    mid_value = (tail_l - tl[3] * head_r) / divisor
    mid_left = tl[2] / divisor
    mid_right = -tl[3] * tr[1] / divisor
    next_value = head_r - tr[0] * mid_value
    next_left = -tr[0] * mid_left
    next_right = tr[1] - tr[0] * mid_right
    return (
        head_l - tl[1] * next_value,
        tail_r - tr[2] * mid_value,
        (
            tl[0] - tl[1] * next_left,
            -tl[1] * next_right,
            -tr[2] * mid_left,
            tr[3] - tr[2] * mid_right,
        ),
    )


def interface_rows(members, me, n):
    zero = jnp.zeros_like(members[0][0])
    identity = (zero, zero, (zero, zero - 1.0, zero - 1.0, zero))

    def choose(cond, a, b):
        return jax.tree.map(lambda x, y: jnp.where(cond, x, y), a, b)

    prefix = identity
    own = members[0]
    for k in range(n):
        own = choose(k == me, members[k], own)
        prefix = choose(k < me, join_slabs(prefix, members[k]), prefix)
    suffix = identity
    for k in range(n - 1, -1, -1):
        suffix = choose(k > me, join_slabs(members[k], suffix), suffix)
    combined = join_slabs(own, suffix)
    lower = (prefix[1] - prefix[2][3] * combined[0]) / (1.0 - prefix[2][3] * combined[2][0])
    upper = (suffix[0] - suffix[2][0] * (own[1] - own[2][2] * lower)) / (
        1.0 - suffix[2][0] * own[2][3]
    )
    return lower, upper


SCALE = 48.0


def kernel(
    n, naz, R, NTL, NZL,
    v, rc, ac, rd, out,
    F, FB, HA, LS, LR, Y, YE, Q, QE, SC, SCE, RCF, ACF, BW, PS, PR, RB0, RBE, RBI, TB, MA, MB, KC,
    PHI, PSI, DP, DM, A0, SPK, CF, STB,
    a0_ss, a0_rs, az_ss, az_rs, lh_ss, lh_rs, ax_ss, ax_rs, r0_ss, r0_rs, re_ss, re_rs, ri_ss, ri_rs, t_ss, t_rs,
    v_s, rb_s, cb_s, o_s,
):
    me = lax.axis_index("rad")
    az = lax.axis_index("az")
    ax = lax.axis_index("ax")
    left = lax.rem(az + naz - 1, naz)
    right = lax.rem(az + 1, naz)
    other = 1 - ax
    near, far = 1 - ax, ax
    peers = [lax.rem(me + d, n) for d in range(1, n)]
    GI = (NTL - 4) // 4
    parity = lax.rem(az, 2)

    def group(k, q):
        lowest = (2, 2 + 3 * GI, 2 + GI, 2 + 2 * GI)
        return lowest[k] if q == 0 else lowest[k ^ 1]

    def edge(p, q):
        return (NTL - 2) * ((p % 2) ^ q)

    first_of = [group(k, 0) + parity * (group(k, 1) - group(k, 0)) for k in range(4)]
    edge_first = [edge(p, 0) + parity * (edge(p, 1) - edge(p, 0)) for p in range(2)]
    side_of = [p + parity * (1 - 2 * p) for p in range(2)]
    beside = [lax.rem(az + naz - 1 + 2 * side_of[p], naz) for p in range(2)]
    bf = jnp.bfloat16

    def v_copy(t, j):
        return pltpu.make_async_copy(
            v.at[:, j, pl.ds(128 * t, 128)], F.at[0, t, j + 2, pl.ds(PAD, R), :], v_s.at[t, j])

    def o_copy(t, j):
        return pltpu.make_async_copy(
            F.at[STEPS % 2, t, j + 2, pl.ds(PAD, R), :],
            out.at[:, j, pl.ds(pl.multiple_of(128 * t, 128), 128)], o_s.at[t, j])

    barrier = pltpu.get_barrier_semaphore()
    for p in peers:
        pl.semaphore_signal(barrier, inc=1, device_id={"rad": p}, device_id_type=MESH)
    for p in (left, right):
        pl.semaphore_signal(barrier, inc=1, device_id={"az": p}, device_id_type=MESH)
    pl.semaphore_signal(barrier, inc=1, device_id={"ax": other}, device_id_type=MESH)

    edges = (0, 1, NTL - 2, NTL - 1)
    for j in edges:
        for t in range(2):
            v_copy(t, j).start()
    row_copies = [
        pltpu.make_async_copy(v.at[r], RB0.at[me, pl.ds(q * NTL, NTL), :], rb_s.at[q])
        for q, r in enumerate((0, R - 1))]
    for c in row_copies:
        c.start()
    for j in range(2, NTL - 2):
        for t in range(2):
            v_copy(t, j).start()
    coef_copies = [
        pltpu.make_async_copy(src, STB.at[q], cb_s.at[q]) for q, src in enumerate((rc, ac))]
    for c in coef_copies:
        c.start()

    row = lax.broadcasted_iota(jnp.int32, (R, 128), 0)
    spacing = 1.0 / (NR + 1)
    radius = 1.0 + ((me * R + row).astype(F32) + 1.0) * spacing
    rdiff = jnp.transpose(jnp.broadcast_to(
        jnp.concatenate([rd[...]] * (128 // R), axis=1), (128, 128)))[0:R, :]
    inward = rdiff * (radius - 0.5 * spacing) / radius
    outward = rdiff * (radius + 0.5 * spacing) / radius
    sink = rdiff * spacing * spacing / (radius * radius)
    grow = 1.0 + sink
    KC[0] = inward
    KC[1] = outward
    KC[2] = grow / outward
    KC[3] = -1.0 / radius
    KC[4] = 1.0 / (radius * radius)
    KC[5] = inward / outward
    KC[6] = grow / inward
    KC[7] = outward / inward
    A0[...] = 66.0 - 30.0 * KC[4]

    lane1 = lax.broadcasted_iota(jnp.int32, (1, 128), 1)
    ones = jnp.ones((1, 128), F32)

    def march(i, carry):
        phi, p, psi, m = carry
        k = R - 1 - i
        PHI[pl.ds(i, 1), :] = phi
        PSI[pl.ds(k, 1), :] = psi
        DM[pl.ds(k, 1), :] = m
        p = KC[2, pl.ds(i, 1), :] * phi + KC[5, pl.ds(i, 1), :] * p
        m = KC[6, pl.ds(k, 1), :] * psi + KC[7, pl.ds(k, 1), :] * m
        DP[pl.ds(i, 1), :] = p
        return phi + p, p, psi + m, m

    lax.fori_loop(0, R, march, (ones, ones, ones, ones))
    weight = 1.0 / (KC[1] * (DP[...] * PSI[...] + PHI[...] * DM[...]))
    at_i = lax.broadcasted_iota(jnp.int32, (R, R), 0)
    at_j = lax.broadcasted_iota(jnp.int32, (R, R), 1)
    upper_part = jnp.transpose(PSI[...] * weight)[0:R, :]
    lower_part = jnp.transpose(PHI[...] * weight)[0:R, :]
    inverse = jnp.where(at_i <= at_j, PHI[:, 0:R] * upper_part, PSI[:, 0:R] * lower_part)
    SPK[0] = -KC[0, 0:1, :] * jnp.broadcast_to(inverse[:, 0:1], (R, 128))
    SPK[1] = -KC[1, R - 1 : R, :] * jnp.broadcast_to(inverse[:, R - 1 : R], (R, 128))
    inverse = inverse * (1.0 / SCALE)
    high = inverse.astype(bf)
    MA[:, 0:R] = high
    MA[:, R : 2 * R] = high
    MB[...] = (inverse - high.astype(F32)).astype(bf)
    TB[me, 0:1, :] = SPK[0, 0:1, :]
    TB[me, 1:2, :] = SPK[1, 0:1, :]
    TB[me, 2:3, :] = SPK[0, R - 1 : R, :]
    TB[me, 3:4, :] = SPK[1, R - 1 : R, :]
    TB[me, 4:8, :] = jnp.zeros((4, 128), F32)
    pl.semaphore_wait(barrier, n + 2)

    def tile_of(p):
        return near if p < 2 else far

    def az_first(p):
        e = p % 2
        return pltpu.make_async_remote_copy(
            src_ref=F.at[0, tile_of(p), pl.ds(edge_first[e] + 2, 2), pl.ds(PAD, R), :],
            dst_ref=F.at[0, tile_of(p), pl.ds((1 - side_of[e]) * (NTL + 2), 2), pl.ds(PAD, R), :],
            send_sem=a0_ss.at[p], recv_sem=a0_rs.at[p], device_id={"az": beside[e]},
            device_id_type=MESH)

    def az_copy(s, p):
        return pltpu.make_async_remote_copy(
            src_ref=YE.at[s - 1, p], dst_ref=HA.at[s - 1, p], send_sem=az_ss.at[s - 1, p],
            recv_sem=az_rs.at[s - 1, p], device_id={"az": beside[p % 2]},
            device_id_type=MESH)

    def lh_copy(s, p):
        return pltpu.make_async_remote_copy(
            src_ref=LS.at[s - 1, p], dst_ref=LR.at[s - 1, p], send_sem=lh_ss.at[s - 1, p],
            recv_sem=lh_rs.at[s - 1, p], device_id={"az": beside[p % 2]},
            device_id_type=MESH)

    def ax_copy(s, m):
        return pltpu.make_async_remote_copy(
            src_ref=PS.at[s, m], dst_ref=PR.at[s, m], send_sem=ax_ss.at[s, m],
            recv_sem=ax_rs.at[s, m], device_id={"ax": other}, device_id_type=MESH)

    def rad_send(buf, ss, rs, d):
        return pltpu.make_async_remote_copy(
            src_ref=buf.at[me], dst_ref=buf.at[me], send_sem=ss.at[d],
            recv_sem=rs.at[me], device_id={"rad": peers[d]}, device_id_type=MESH)

    def rad_recv(buf, ss, rs, d):
        return pltpu.make_async_remote_copy(
            src_ref=buf.at[me], dst_ref=buf.at[peers[d]], send_sem=ss.at[d],
            recv_sem=rs.at[peers[d]], device_id={"rad": peers[d]}, device_id_type=MESH)

    for j in edges:
        for t in range(2):
            v_copy(t, j).wait()
    for p in range(4):
        az_first(p).start()
    for c in row_copies:
        c.wait()
    for d in range(n - 1):
        rad_send(RB0, r0_ss, r0_rs, d).start()
        rad_send(TB, t_ss, t_rs, d).start()

    lane = lax.broadcasted_iota(jnp.int32, (CH, 128), 1)

    def members_of(m):
        if m is None:
            return [x for q in range(4) for x in members_of(q)]
        inner = [first_of[m] + i for i in range(GI)]
        layers = ([edge_first[m], edge_first[m] + 1] if m < 2 else []) + inner
        first = m * GI + 2 * min(m, 2)
        return [(first + i, j) for i, j in enumerate(layers)]

    def pack(s, m):
        b = lax.rem(s, 2)
        for c in range(R // CH):
            acc = jnp.zeros((CH, 128), F32)
            for i, j in members_of(m):
                edge = F[b, near, j + 2, pl.ds(PAD + c * CH, CH), :]
                acc = jnp.where(lane // 2 == i, pltpu.roll(edge, 2 * i + 2 * (1 - ax), 1), acc)
            PS[s, m or 0, pl.ds(c * CH, CH), :] = acc

    def unpack(s, m):
        for c in range(R // CH):
            rows = pl.ds(c * CH, CH)
            x = PR[s, jnp.where(s == 0, 0, m), rows, :]
            high = x.astype(bf).astype(F32)
            x = jnp.where(lane < 64, high, pltpu.roll(x - high, 64, 1))
            for i, j in members_of(m):
                FB[j, rows, pl.ds(512, 128)] = jnp.where((lane % 64) // 2 == i, x, 0.0).astype(bf)

    def split_store(j, rows, t, x):
        high = x.astype(bf)
        at = pl.multiple_of(t * 128, 128) if not isinstance(t, int) else t * 128
        FB[j, rows, pl.ds(at, 128)] = high
        FB[j, rows, pl.ds(256 + at, 128)] = (x - high.astype(F32)).astype(bf)

    for j in range(2, NTL - 2):
        for t in range(2):
            v_copy(t, j).wait()

    def first_split(j, carry):
        for t in range(2):
            for c in range(R // CH):
                rows = pl.ds(c * CH, CH)
                split_store(j, rows, t, F[0, t, j + 2, pl.ds(PAD + c * CH, CH), :])
        return carry

    pack(0, None)
    ax_copy(0, 0).start()
    lax.fori_loop(0, NTL, first_split, 0)

    def band(source, t):
        d = source - (128 * t + lax.broadcasted_iota(jnp.int32, (CH, 128), 1))
        slope = (jnp.where(d == 1, -32.0, 0.0) + jnp.where(d == -1, 32.0, 0.0)
                 + jnp.where(d == 2, 4.0, 0.0) + jnp.where(d == -2, -4.0, 0.0))
        curve = (jnp.where(jnp.abs(d) == 1, 16.0, 0.0) - jnp.where(jnp.abs(d) == 2, 1.0, 0.0))
        return slope.astype(bf), curve.astype(bf)

    here = lax.broadcasted_iota(jnp.int32, (CH, 128), 0)

    def bands(c, carry):
        r0 = pl.multiple_of(c * CH, CH)
        for t in range(2):
            slope, curve = band(here + c * CH, t)
            for q in range(2):
                BW[t, pl.ds(pl.multiple_of(q * 256 + r0, CH), CH), 0:128] = slope
                BW[t, pl.ds(pl.multiple_of(q * 256 + r0, CH), CH), 128:256] = curve
        return carry

    lax.fori_loop(0, 256 // CH, bands, 0)
    for t in range(2):
        slope, curve = band(jnp.where(ax == 0, 256 + here % 2, here % 2 - 2), t)
        for c in range(128 // CH):
            BW[t, pl.ds(512 + c * CH, CH), 0:128] = slope
            BW[t, pl.ds(512 + c * CH, CH), 128:256] = curve

    for q, (dst, scale) in enumerate(((RCF, -0.5 * SCALE), (ACF, None))):
        coef_copies[q].wait()
        for t in range(2):
            def convert(c, carry):
                rows = pl.ds(pl.multiple_of(c * 8, 8), 8)
                x = STB[q, rows, :, pl.ds(128 * t, 128)].astype(F32)
                dst[t, :, rows, :] = jnp.swapaxes(x if scale is None else x * scale, 0, 1)
                return carry

            lax.fori_loop(0, R // 8, convert, 0)

    for d in range(n - 1):
        rad_recv(RB0, r0_ss, r0_rs, d).wait_recv()
    below = jnp.maximum(me - 1, 0)
    above = jnp.minimum(me + 1, n - 1)
    low0 = jnp.where(me > 0, RB0[below, NTL : 2 * NTL, :], 0.0)
    high0 = jnp.where(me < n - 1, RB0[above, 0:NTL, :], 0.0)
    for j in range(NTL):
        for t in range(2):
            F[0, t, j + 2, PAD - 1 : PAD, :] = low0[j : j + 1, 128 * t : 128 * t + 128]
            F[0, t, j + 2, PAD + R : PAD + R + 1, :] = high0[j : j + 1, 128 * t : 128 * t + 128]

    for d in range(n - 1):
        rad_recv(TB, t_ss, t_rs, d).wait_recv()
    members = []
    for k in range(n):
        members.append((
            jnp.where(lane1 == 2 * k, 1.0, 0.0),
            jnp.where(lane1 == 2 * k + 1, 1.0, 0.0),
            tuple(TB[k, q : q + 1, :] for q in range(4)),
        ))
    lower_map, upper_map = interface_rows(members, me, n)
    for m in range(2 * n):
        for h, vec in enumerate((lower_map, upper_map)):
            val = jnp.sum(jnp.where(lane1 == m, vec, 0.0), axis=1, keepdims=True)
            CF[h, m // 2, m % 2 : m % 2 + 1, :] = jnp.broadcast_to(val, (1, 128))

    def right_side(b, t, j, r0, near_by, slope, curve):
        rows = pl.ds(PAD + r0, CH)
        at = pl.ds(r0, CH)
        f = F[b, t, j + 2, rows, :]
        lo = F[b, t, j + 2, pl.ds(PAD + r0 - 1, CH), :]
        up = F[b, t, j + 2, pl.ds(PAD + r0 + 1, CH), :]
        m2, m1, p1, p2 = near_by
        dt = 8.0 * (p1 - m1) - (p2 - m2)
        lt = 16.0 * (p1 + m1) - (p2 + m2)
        return (
            f * (A0[at, :] + KC[3, at, :] * dt) + KC[4, at, :] * lt
            + RCF[t, j, at, :] * (up - lo) + (ACF[t, j, at, :] * slope + curve)
        )

    def solve(q):
        return (jnp.dot(MA[...], q[...], preferred_element_type=F32)
                + jnp.dot(MB[...], q[0:R, :], preferred_element_type=F32))

    def put_q(q, r0, cols, x):
        high = x.astype(bf)
        q[pl.ds(r0, CH), cols] = high
        q[pl.ds(R + r0, CH), cols] = (x - high.astype(F32)).astype(bf)

    def stencil(dst, lhs):
        dst[near] = jnp.dot(lhs, BW[near], preferred_element_type=F32)
        dst[far] = jnp.dot(lhs[:, 0:512], BW[far, 0:512, :], preferred_element_type=F32)

    def ax_wait(s, m):
        if m == 0:
            ax_copy(s, m).wait()
        else:
            @pl.when(s > 0)
            def _():
                ax_copy(s, m).wait()

    def axial(s, k):
        unpack(s, k)
        stencil(SC, FB[pl.ds(first_of[k], GI)].reshape(GI * R, 640))

    def axial_edges(k):
        stencil(SCE.at[k], FB[pl.ds(edge_first[k], 2)].reshape(2 * R, 640))

    def edge_solve(s, p):
        side = p % 2
        b = lax.rem(s, 2)
        t = tile_of(p)

        halo = side_of[side] * (NTL + 2)

        @pl.when(s == 0)
        def _():
            az_first(p).wait_recv()

        @pl.when(s > 0)
        def _():
            for copy in (az_copy, lh_copy):
                copy(s, p).wait_recv()
            for i in range(2):
                cols = slice(i * 128, i * 128 + 128)
                low = LR[s - 1, p, 0:1, cols]
                high = LR[s - 1, p, 1:2, cols]
                for c in range(R // CH):
                    here = pl.ds(c * CH, CH)
                    rows = pl.ds(PAD + c * CH, CH)
                    F[b, t, halo + i, rows, :] = (
                        HA[s - 1, p, here, cols] - SPK[0, here, :] * low
                        - SPK[1, here, :] * high - F[1 - b, t, halo + i, rows, :])

        for i in range(2):
            j = edge_first[side] + i
            for c in range(R // CH):
                r0 = c * CH
                at = pl.ds(i * R + r0, CH)
                x = right_side(
                    b, t, j, r0,
                    [F[b, t, j + 2 + o, pl.ds(PAD + r0, CH), :] for o in (-2, -1, 1, 2)],
                    SCE[side, t, at, 0:128], SCE[side, t, at, 128:256])
                put_q(QE, r0, pl.ds(i * 128, 128), x)
        y = solve(QE)
        YE[s, p] = y

        @pl.when(s < STEPS - 1)
        def _():
            az_copy(s + 1, p).start()

        RBE[s, p, me, 0:1, :] = y[0:1, :]
        RBE[s, p, me, 1:2, :] = y[R - 1 : R, :]
        for d in range(n - 1):
            rad_send(RBE.at[s, p], re_ss.at[s, p], re_rs.at[s, p], d).start()

    def ends(buf, idx, width):
        res = []
        for h in range(2):
            total = None
            for k in range(n):
                coef = jnp.concatenate([CF[h, k]] * (width // 128), axis=1)
                term = coef * buf[(*idx, k)]
                total = term if total is None else total + term
            res.append(total[0:1, :] + total[1:2, :])
        return res

    def advance(b, t, j, y_of, low, high):
        for c in range(R // CH):
            here = pl.ds(c * CH, CH)
            rows = pl.ds(PAD + c * CH, CH)
            x = (y_of(here) - SPK[0, here, :] * low - SPK[1, here, :] * high - F[b, t, j + 2, rows, :])
            F[1 - b, t, j + 2, rows, :] = x
            split_store(j, here, t, x)
        F[1 - b, t, j + 2, PAD - 1 : PAD, :] = low - F[b, t, j + 2, PAD - 1 : PAD, :]
        F[1 - b, t, j + 2, PAD + R : PAD + R + 1, :] = high - F[b, t, j + 2, PAD + R : PAD + R + 1, :]

    def edge_finish(s, p):
        b = lax.rem(s, 2)
        t = tile_of(p)
        buf, ss, rs = RBE.at[s, p], re_ss.at[s, p], re_rs.at[s, p]
        for d in range(n - 1):
            rad_send(buf, ss, rs, d).wait_send()
        for d in range(n - 1):
            rad_recv(buf, ss, rs, d).wait_recv()
        low, high = ends(RBE, (s, p), 256)

        @pl.when(s == 0)
        def _():
            az_first(p).wait_send()

        @pl.when(s > 0)
        def _():
            az_copy(s, p).wait_send()
            lh_copy(s, p).wait_send()

        @pl.when(s < STEPS - 1)
        def _():
            LS[s, p, 0:1, :] = low
            LS[s, p, 1:2, :] = high
            lh_copy(s + 1, p).start()

        for i in range(2):
            cols = slice(i * 128, i * 128 + 128)
            advance(b, t, edge_first[p % 2] + i,
                    lambda here: YE[s, p, here, cols], low[:, cols], high[:, cols])

        for q in range(2):
            @pl.when(jnp.logical_and(s == STEPS - 1, parity == q))
            def _():
                for i in range(2):
                    o_copy(t, edge(p, q) + i).start()

    def inner_solve(s, k):
        b = lax.rem(s, 2)
        def rhs(i):
            j = first_of[k] + i
            for c in range(R // CH):
                for t in range(2):
                    r0 = c * CH
                    at = pl.ds(pl.multiple_of(i * R + r0, CH), CH)
                    x = right_side(
                        b, t, j, r0,
                        [F[b, t, j + 2 + o, pl.ds(PAD + r0, CH), :] for o in (-2, -1, 1, 2)],
                        SC[t, at, 0:128], SC[t, at, 128:256])
                    put_q(Q.at[i], r0, pl.ds(t * 128, 128), x)

        def close(i):
            y = solve(Q.at[i])
            Y[k, i] = y
            cols = pl.ds(pl.multiple_of(i * NZL, NZL), NZL)
            RBI[s, k, me, 0:1, cols] = y[0:1, :]
            RBI[s, k, me, 1:2, cols] = y[R - 1 : R, :]

        rhs(0)

        def body(i, c):
            close(i - 1)
            rhs(i)
            return c

        lax.fori_loop(1, GI, body, 0)
        close(GI - 1)
        for d in range(n - 1):
            rad_send(RBI.at[s, k], ri_ss.at[s, k], ri_rs.at[s, k], d).start()

    def inner_finish(s, k, then=None):
        b = lax.rem(s, 2)
        buf, ss, rs = RBI.at[s, k], ri_ss.at[s, k], ri_rs.at[s, k]
        for d in range(n - 1):
            rad_send(buf, ss, rs, d).wait_send()
        if then is not None:
            ax_wait(*then)
        for d in range(n - 1):
            rad_recv(buf, ss, rs, d).wait_recv()
        if then is not None:
            axial(*then)
        low, high = ends(RBI, (s, k), GI * NZL)
        for i in range(GI):
            for t in range(2):
                cols = slice(i * NZL + t * 128, i * NZL + t * 128 + 128)
                advance(b, t, first_of[k] + i,
                        lambda here: Y[k, i, here, pl.ds(t * 128, 128)],
                        low[:, cols], high[:, cols])

        for q in range(2):
            @pl.when(jnp.logical_and(s == STEPS - 1, parity == q))
            def _():
                for i in range(GI):
                    for t in range(2):
                        o_copy(t, group(k, q) + i).start()

    def send_axial(s, k):
        pack(s, k)
        ax_copy(s, k).start()

    def step(s, carry):
        for k in range(4):
            inner_solve(s, k)
            edge_solve(s, k)
            if k == 0:
                @pl.when(s > 0)
                def _():
                    edge_finish(s - 1, 3)
                    inner_finish(s - 1, 3, (s, 1))
                    send_axial(s, 3)

                @pl.when(s == 0)
                def _():
                    axial(s, 1)

                axial_edges(1)
            elif k < 3:
                edge_finish(s, k - 1)
                inner_finish(s, k - 1, (s, k + 1))

                @pl.when(s < STEPS - 1)
                def _():
                    send_axial(s + 1, k - 1)
            else:
                @pl.when(s < STEPS - 1)
                def _():
                    inner_finish(s, 2, (s + 1, 0))

                @pl.when(s == STEPS - 1)
                def _():
                    inner_finish(s, 2)

                edge_finish(s, 2)

                @pl.when(s < STEPS - 1)
                def _():
                    send_axial(s + 1, 2)
                    axial_edges(0)
        return carry

    ax_wait(0, 0)
    axial(0, 0)
    axial_edges(0)
    lax.fori_loop(0, STEPS, step, 0)
    inner_finish(STEPS - 1, 3)
    edge_finish(STEPS - 1, 3)
    for j in range(NTL):
        for t in range(2):
            o_copy(t, j).wait()
    for d in range(n - 1):
        rad_send(RB0, r0_ss, r0_rs, d).wait_send()
        rad_send(TB, t_ss, t_rs, d).wait_send()


def local(n, naz, velocity, radial_courant, axial_courant, radial_diffusion):
    R, NTL, NZL = velocity.shape
    S = STEPS
    GI = (NTL - 4) // 4
    dma = pltpu.SemaphoreType.DMA
    bf = jnp.bfloat16
    hbm = pl.BlockSpec(memory_space=pl.ANY)
    return pl.pallas_call(
        functools.partial(kernel, n, naz, R, NTL, NZL),
        out_shape=jax.ShapeDtypeStruct((R, NTL, NZL), F32),
        in_specs=[hbm, hbm, hbm, pl.BlockSpec(memory_space=pltpu.VMEM)],
        out_specs=hbm,
        scratch_shapes=[
            pltpu.VMEM((2, 2, NTL + 4, R + 2 * PAD, 128), F32),
            pltpu.VMEM((NTL, R, 640), bf),
            pltpu.VMEM((S - 1, 4, R, 256), F32),
            pltpu.VMEM((S - 1, 4, 2, 256), F32),
            pltpu.VMEM((S - 1, 4, 2, 256), F32),
            pltpu.VMEM((4, GI, R, NZL), F32),
            pltpu.VMEM((S, 4, R, 256), F32),
            pltpu.VMEM((GI, 2 * R, NZL), bf),
            pltpu.VMEM((2 * R, 256), bf),
            pltpu.VMEM((2, GI * R, 256), F32),
            pltpu.VMEM((2, 2, 2 * R, 256), F32),
            pltpu.VMEM((2, NTL, R, 128), F32),
            pltpu.VMEM((2, NTL, R, 128), F32),
            pltpu.VMEM((2, 640, 256), bf),
            pltpu.VMEM((S, 4, R, 128), F32),
            pltpu.VMEM((S, 4, R, 128), F32),
            pltpu.VMEM((n, 2 * NTL, NZL), F32),
            pltpu.VMEM((S, 4, n, 2, 256), F32),
            pltpu.VMEM((S, 4, n, 2, GI * NZL), F32),
            pltpu.VMEM((n, 8, 128), F32),
            pltpu.VMEM((R, 2 * R), bf),
            pltpu.VMEM((R, R), bf),
            pltpu.VMEM((8, R, 128), F32),
            pltpu.VMEM((R, 128), F32),
            pltpu.VMEM((R, 128), F32),
            pltpu.VMEM((R, 128), F32),
            pltpu.VMEM((R, 128), F32),
            pltpu.VMEM((R, 128), F32),
            pltpu.VMEM((2, R, 128), F32),
            pltpu.VMEM((2, n, 2, 128), F32),
            pltpu.VMEM((2, R, NTL, NZL), bf),
            dma((4,)), dma((4,)), dma((S - 1, 4)), dma((S - 1, 4)), dma((S - 1, 4)), dma((S - 1, 4)),
            dma((S, 4)), dma((S, 4)),
            dma((n,)), dma((n,)), dma((S, 4, n)), dma((S, 4, n)),
            dma((S, 4, n)), dma((S, 4, n)), dma((n,)), dma((n,)),
            dma((2, NTL)), dma((2,)), dma((2,)), dma((2, NTL)),
        ],
        compiler_params=pltpu.CompilerParams(
            collective_id=0, has_side_effects=True, vmem_limit_bytes=58 * 1024 * 1024),
    )(velocity, radial_courant, axial_courant, radial_diffusion.reshape(1, R))


def solution(mesh):
    return jax.shard_map(
        functools.partial(local, mesh.shape["rad"], mesh.shape["az"]),
        mesh=mesh,
        in_specs=(P("rad", "az", "ax"), P("rad", "az", "ax"), P("rad", "az", "ax"), P("rad")),
        out_specs=P("rad", "az", "ax"),
        check_vma=False,
    )
```
